512 devices in a mesh: wide: 64 (over y, z), tp: 8 (over x, core).
Axes of the slice: x: 4, y: 4, z: 16, core: 2. Of those that a mesh axis runs over, the one named last changes fastest.
Arguments:
- hidden: bfloat16 [256, 2, 4096], P('wide'), may hold values from -6 to 6
- new_keys: bfloat16 [256, 2, 1024], P('wide', None, 'tp'), may hold values from -6 to 6
- key_cache: bfloat16 [256, 8, 512, 128], P('wide', 'tp'), may hold values from -700 to 700
- value_cache: bfloat16 [256, 8, 512, 128], P('wide', 'tp'), may hold values from -6 to 6
- cache_len: int32 [256], P('wide'), may hold values from 1 to 512
- adapter_id: int32 [256], P('wide'), may hold values from 0 to 255
- adapter_slot: int32 [256], replicated, may hold values from 0 to 255, each once
- adapter_rank: int32 [256], replicated, may hold values from 1 to 64
- q_weight: bfloat16 [4096, 2048], P(None, 'tp'), may hold values from -0.09375 to 0.09375
- v_weight: bfloat16 [4096, 1024], P(None, 'tp'), may hold values from -0.09375 to 0.09375
- q_down: bfloat16 [256, 4096, 64], P('wide', 'tp'), may hold values from -0.09375 to 0.09375
- v_down: bfloat16 [256, 4096, 64], P('wide', 'tp'), may hold values from -0.09375 to 0.09375
- q_up: bfloat16 [256, 64, 2048], P('wide', None, 'tp'), may hold values from -1 to 1
- v_up: bfloat16 [256, 64, 1024], P('wide', None, 'tp'), may hold values from -1 to 1
Outputs:
- attended: bfloat16 [256, 2, 2048], P('wide', None, 'tp')
- new_values: bfloat16 [256, 2, 1024], P('wide', None, 'tp')
The draws below stay inside these ranges and needn't reach their ends.
Inputs may be any that keep to these rules, and one draw needn't show every extreme that they name: Adapter a is stored at slot adapter_slot[a], on the index adapter_slot[a] // 4 of wide, at position adapter_slot[a] % 4 there. Only the first adapter_rank[a] of the 64 columns of an adapter's first factors, and rows of its second factors, belong to it. The new tokens stand at positions cache_len and cache_len + 1.
All inputs are finite; a program needn't handle non-finite values.
Results may differ from the reference program's by a relative error of at most 0.014.
The reference program's roundings to bfloat16 on the way count: a program that leaves them out, or rounds other values in their place, can miss the bound.
Values may be sent and summed in bfloat16 or wider, within the bound.
A program may use at most 64 MiB of HBM per device.

```python
import math
import jax
import jax.numpy as jnp
import numpy as np
from jax import lax

D = 4096
HEADS = 16
KV_HEADS = 8
HD = 128
CACHE = 512
RANK = 64
ADAPTERS = 256
ROWS = 256


def draw_key_cache(key, part):
    base = jnp.clip(jax.random.normal(key, (ROWS, KV_HEADS, CACHE, HD), jnp.float32), -6.0, 6.0)
    return base.astype(jnp.bfloat16)


def plant(array, rng, smallest, high):
    spot = [jax.random.randint(jax.random.fold_in(rng, axis), (), 0, length) for axis, length in enumerate(array.shape)]
    widest = array.shape.index(max(array.shape))
    neighbour = spot[:widest] + [(spot[widest] + 1) % array.shape[widest]] + spot[widest + 1:]
    return array.at[tuple(spot)].set(smallest).at[tuple(neighbour)].set(high)


def block_levels(stream_key, extent, pieces, least, high):
    factor_of = 1.0
    for dim, blocks in pieces:
        steps = jax.random.uniform(jax.random.fold_in(jax.random.fold_in(stream_key, 6), dim), (blocks,), jnp.float32, least / len(pieces), high / len(pieces))
        factor_of = factor_of * jnp.repeat(jnp.exp(steps), extent[dim] // blocks).reshape((-1,) + (1,) * (len(extent) - 1 - dim))
    return factor_of


def rank_table(number_of, lean):
    portions = [(1 << 20) // math.isqrt(grade ** lean) + 1 for grade in range(1, number_of + 1)]
    scale = 1 + sum(portions) // (1 << 30)
    return np.cumsum(np.array([max(1, weight // scale) for weight in portions]))


def ranked_ids(rng, dims, count, lean):
    grid = rank_table(count, lean)
    ticket = jax.random.randint(jax.random.fold_in(rng, 1), dims, 0, int(grid[count - 1]))
    rank = jnp.searchsorted(jnp.asarray(grid, jnp.int32), ticket, side="right")
    return jax.random.permutation(jax.random.fold_in(rng, 2), count)[rank].astype(jnp.int32)


def centred(stream_key, shape, scale, reach, pieces=(), held_as=jnp.bfloat16):
    factor_of = block_levels(stream_key, shape, pieces, -0.22, 0.18) if pieces else 1.0
    entries = jax.random.normal(stream_key, shape, jnp.float32) * scale * factor_of
    return jnp.minimum(jnp.maximum(entries, -reach), reach).astype(held_as)


def setup_inputs(seed: int = 0) -> dict:
    key_of = jax.random.split(jax.random.key(seed), 15)
    hidden = centred(key_of[0], (ROWS, 2, D), 1.0, 6.0, ((0, 64),))
    new_keys = centred(key_of[1], (ROWS, 2, KV_HEADS * HD), 1.0, 6.0, ((0, 64), (2, 8)))
    key_cache = draw_key_cache(jax.random.fold_in(key_of[14], 71), 0)
    value_cache = centred(key_of[3], (ROWS, KV_HEADS, CACHE, HD), 1.0, 6.0, ((0, 64), (1, 8)))
    cache_len = plant(jax.random.randint(key_of[4], (ROWS,), 1, CACHE + 1), jax.random.fold_in(key_of[4], 1), 1, CACHE).astype(jnp.int32)
    adapter_id = plant(ranked_ids(key_of[5], (ROWS,), ADAPTERS, 2), jax.random.fold_in(key_of[5], 3), 0, ADAPTERS - 1).astype(jnp.int32)
    adapter_slot = jax.random.permutation(key_of[6], ADAPTERS).astype(jnp.int32)
    adapter_rank = plant(jax.random.randint(key_of[7], (ADAPTERS,), 1, RANK + 1), jax.random.fold_in(key_of[7], 1), 1, RANK).astype(jnp.int32)
    q_weight = centred(key_of[8], (D, HEADS * HD), D ** -0.5, 0.09375, ((1, 8),))
    v_weight = centred(key_of[9], (D, KV_HEADS * HD), D ** -0.5, 0.09375, ((1, 8),))
    q_down = centred(key_of[10], (ADAPTERS, D, RANK), D ** -0.5, 0.09375, ((0, 64), (1, 8)))
    v_down = centred(key_of[11], (ADAPTERS, D, RANK), D ** -0.5, 0.09375, ((0, 64), (1, 8)))
    q_up = centred(key_of[12], (ADAPTERS, RANK, HEADS * HD), (RANK // 2) ** -0.5, 1.0, ((0, 64), (2, 8)))
    v_up = centred(key_of[13], (ADAPTERS, RANK, KV_HEADS * HD), (RANK // 2) ** -0.5, 1.0, ((0, 64), (2, 8)))
    return {"hidden": hidden, "new_keys": new_keys, "key_cache": key_cache, "value_cache": value_cache, "cache_len": cache_len, "adapter_id": adapter_id, "adapter_slot": adapter_slot, "adapter_rank": adapter_rank, "q_weight": q_weight, "v_weight": v_weight, "q_down": q_down, "v_down": v_down, "q_up": q_up, "v_up": v_up}


def rotate(queries, position):
    head_dim = queries.shape[-1]
    half_width = head_dim // 2
    frequency = jnp.exp(-math.log(500000.0) * (2.0 * jnp.arange(half_width, dtype=jnp.float32) / head_dim))
    angles = position.astype(jnp.float32)[:, :, None] * frequency
    cosine = jnp.cos(angles)[:, :, None, :]
    sine_part = jnp.sin(angles)[:, :, None, :]
    lower_half = queries[..., :half_width]
    second = queries[..., half_width:]
    return jnp.concatenate([lower_half * cosine - second * sine_part, second * cosine + lower_half * sine_part], -1)

def attend_row(items):
    queries, fresh_keys, fresh_values, keys_row, values_row, length = items
    inv_root = 1.0 / math.sqrt(queries.shape[-1])
    queries = queries.astype(jnp.float32)
    old_scores = jnp.einsum('sghd,gcd->sghc', queries, keys_row.astype(jnp.float32)) * inv_root
    live_slot = jnp.arange(keys_row.shape[1]) < length
    old_scores = jnp.where(live_slot[None, None, None, :], old_scores, -jnp.inf)
    new_scores = jnp.einsum('sghd,jgd->sghj', queries, fresh_keys.astype(jnp.float32)) * inv_root
    causal = jnp.arange(2)[None, :] <= jnp.arange(2)[:, None]
    new_scores = jnp.where(causal[:, None, None, :], new_scores, -jnp.inf)
    largest = jnp.maximum(lax.optimization_barrier(jnp.max(old_scores, -1)), lax.optimization_barrier(jnp.max(new_scores, -1)))
    old_weight = jnp.exp(old_scores - largest[..., None])
    new_weight = jnp.exp(new_scores - largest[..., None])
    denominator = lax.optimization_barrier(jnp.sum(old_weight, -1)) + lax.optimization_barrier(jnp.sum(new_weight, -1))
    old_prob = (old_weight / denominator[..., None]).astype(jnp.bfloat16)
    new_prob = (new_weight / denominator[..., None]).astype(jnp.bfloat16)
    result = jnp.einsum('sghc,gcd->sghd', old_prob.astype(jnp.float32), values_row.astype(jnp.float32))
    result = result + jnp.einsum('sghj,jgd->sghd', new_prob.astype(jnp.float32), fresh_values.astype(jnp.float32))
    return result.astype(jnp.bfloat16)

def reference(hidden, new_keys, key_cache, value_cache, cache_len, adapter_id, adapter_slot, adapter_rank, q_weight, v_weight, q_down, v_down, q_up, v_up):
    slot_index = adapter_slot[adapter_id]
    rank_value = adapter_rank[adapter_id]

    def adapter_terms(items):
        hidden_row, slot, rank = items
        down_table = jnp.concatenate([q_down[slot], v_down[slot]], 1)
        reduced = jnp.dot(hidden_row, down_table, preferred_element_type=jnp.float32)
        rank_mask = (jnp.arange(RANK) < rank).astype(jnp.float32)
        reduced = (reduced * jnp.concatenate([rank_mask, rank_mask])[None, :]).astype(jnp.bfloat16)
        delta_q = jnp.dot(reduced[:, :RANK], q_up[slot], preferred_element_type=jnp.float32).astype(jnp.bfloat16)
        delta_v = jnp.dot(reduced[:, RANK:], v_up[slot], preferred_element_type=jnp.float32).astype(jnp.bfloat16)
        return (delta_q, delta_v)
    delta_q, delta_v = lax.map(adapter_terms, (hidden, slot_index, rank_value))
    flat_rows = hidden.reshape(ROWS * 2, D)
    queries = jnp.dot(flat_rows, q_weight, preferred_element_type=jnp.float32).reshape(ROWS, 2, HEADS * HD) + delta_q.astype(jnp.float32)
    new_values = jnp.dot(flat_rows, v_weight, preferred_element_type=jnp.float32).reshape(ROWS, 2, KV_HEADS * HD) + delta_v.astype(jnp.float32)
    new_values = new_values.astype(jnp.bfloat16)
    position = cache_len[:, None] + jnp.arange(2, dtype=jnp.int32)[None, :]
    queries = rotate(queries.reshape(ROWS, 2, HEADS, HD), position).astype(jnp.bfloat16)
    queries = queries.reshape(ROWS, 2, KV_HEADS, HEADS // KV_HEADS, HD)
    attended = lax.map(attend_row, (queries, new_keys.reshape(ROWS, 2, KV_HEADS, HD), new_values.reshape(ROWS, 2, KV_HEADS, HD), key_cache, value_cache, cache_len))
    return (attended.reshape(ROWS, 2, HEADS * HD), new_values)
```

```python
import functools
import math

import jax
import jax.numpy as jnp
from jax import lax
from jax.experimental import pallas as pl
from jax.experimental.pallas import tpu as pltpu
from jax.sharding import PartitionSpec as P

MESH = pl.DeviceIdType.MESH
LANES = 128


def factors(wide):
    return (4, 4, wide // 16) if wide >= 32 else (2, 2, wide // 4)


def order_of(n):
    near = [d for d in (1, n - 1) if d < n]
    return list(dict.fromkeys(near + list(range(1, n))))


def kernel(
    dims,
    hidden,
    new_keys,
    key_cache,
    value_cache,
    cache_len,
    adapter_id,
    adapter_slot,
    adapter_rank,
    q_weight,
    v_weight,
    q_down,
    v_down,
    q_up,
    v_up,
    attended,
    new_values,
    hid,
    h32,
    h16,
    kv,
    vv,
    nk,
    len_s,
    id_s,
    slot_s,
    rank_s,
    wq,
    wv,
    down,
    upq,
    upv,
    feats,
    meta,
    locs,
    mixed,
    arrive_p,
    red,
    delta,
    r1,
    s1,
    r2,
    s2,
    r3,
    base,
    cos_t,
    sin_t,
    kn,
    vn,
    local_sem,
    p1_send,
    p1_recv,
    m1_send,
    m1_recv,
    p2_send,
    p2_recv,
    m2_send,
    m2_recv,
    p3_send,
    p3_recv,
    m3_send,
    m3_recv,
    rs_send,
    rs_recv,
    ag_send,
    ag_recv,
    d1_send,
    d1_recv,
    d2_send,
    d2_recv,
    d3_send,
    d3_recv,
):
    ny, nn, nf, nt = dims
    nh = nf // 2
    rows, _, width = hidden.shape
    toks = rows * 2
    part = width // nt
    slots = q_up.shape[0]
    rank_w = q_up.shape[1]
    q_w = q_up.shape[2]
    v_w = v_up.shape[2]
    cache = key_cache.shape[2]
    bf, f32 = jnp.bfloat16, jnp.float32

    wide = lax.axis_index("wide")
    tp = lax.axis_index("tp")
    y = lax.div(wide, nf * nn)
    z = lax.rem(wide, nf * nn)
    zf = lax.div(z, nn)
    zn = lax.rem(z, nn)

    def turn(i, d, n):
        return lax.rem(i + d, n)

    def y_peer(d):
        return (turn(y, d, ny) * (nf * nn) + z, tp)

    def n_peer(d):
        return (y * (nf * nn) + zf * nn + turn(zn, d, nn), tp)

    def f_peer(d):
        return (y * (nf * nn) + turn(zf, d, nf) * nn + zn, tp)

    def t_peer(d):
        return (wide, turn(tp, d, nt))

    a_of = (y, zn)
    b_of = (zn, y)
    a_peer = (y_peer, n_peer)
    b_peer = (n_peer, y_peer)
    n_ab = ny

    loads = {}

    def load(name, src, dst, i):
        c = pltpu.make_async_copy(src, dst, local_sem.at[i])
        c.start()
        loads[name] = c

    load("hid", hidden, hid, 0)
    load("id", adapter_id, id_s, 1)
    load("slot", adapter_slot, slot_s, 2)
    load("rank", adapter_rank, rank_s, 3)
    load("len", cache_len, len_s, 4)
    load("nk", new_keys, nk, 5)

    barrier = pltpu.get_barrier_semaphore()
    peers = (
        [f_peer(d) for d in range(1, nf)]
        + [n_peer(d) for d in range(1, nn)]
        + [y_peer(d) for d in range(1, ny)]
        + [t_peer(d) for d in range(1, nt)]
    )
    for p in peers:
        pl.semaphore_signal(barrier, inc=1, device_id=p, device_id_type=MESH)

    for k in range(slots):
        row = k * 2 * rank_w
        load(f"qd{k}", q_down.at[k], down.at[pl.ds(row, rank_w)], 8 + 4 * k)
        load(f"vd{k}", v_down.at[k], down.at[pl.ds(row + rank_w, rank_w)], 9 + 4 * k)
    load("wq", q_weight, wq, 6)
    load("wv", v_weight, wv, 7)
    upq[...] = jnp.zeros_like(upq)
    upv[...] = jnp.zeros_like(upv)
    for k in range(slots):
        row = k * 2 * rank_w
        load(f"qu{k}", q_up.at[k], upq.at[pl.ds(row, rank_w)], 10 + 4 * k)
        load(f"vu{k}", v_up.at[k], upv.at[pl.ds(row + rank_w, rank_w)], 11 + 4 * k)
    n0 = 8 + 4 * slots
    load("kc", key_cache, kv, n0)
    load("vc", value_cache, vv, n0 + 1)

    own_set = lax.div(zf, nh)
    own_h = lax.rem(zf, nh)
    own_a = jnp.where(own_set == 0, y, zn)
    own_b = jnp.where(own_set == 0, zn, y)
    loads["hid"].wait()
    for r in range(rows):
        col = pl.multiple_of(tp * part, part)
        h32[2 * r : 2 * r + 2, :part] = hid[r, :, pl.ds(col, part)].astype(f32)
    feats[own_set, own_a, own_b, own_h] = h32[:, :part].astype(bf)
    for name in ("id", "slot", "rank", "len"):
        loads[name].wait()
    lane1 = lax.broadcasted_iota(jnp.int32, (1, LANES), 1)
    code = jnp.zeros((1, LANES), jnp.int32)
    for r in range(rows):
        ident = id_s[r]
        code = jnp.where(lane1 == r, slot_s[ident] * 256 + rank_s[ident], code)
    meta[own_set, own_a, own_b, own_h] = code

    sends = []

    def send(src, dst, ssem, rsem, peer):
        c = pltpu.make_async_remote_copy(
            src_ref=src,
            dst_ref=dst,
            send_sem=ssem,
            recv_sem=rsem,
            device_id=peer,
            device_id_type=MESH,
        )
        c.start()
        sends.append(c)

    def arrived(ref, sem):
        pltpu.make_async_copy(ref, ref, sem).wait()

    pl.semaphore_wait(barrier, len(peers))

    own = (own_set, own_a, own_b, own_h)
    for d in order_of(nf):
        send(meta.at[own], meta.at[own], m1_send.at[d], m1_recv.at[d], f_peer(d))
        send(feats.at[own], feats.at[own], p1_send.at[d], p1_recv.at[d], f_peer(d))

    for r in range(rows):
        h32[2 * r : 2 * r + 2, :] = hid[r].astype(f32)
    h16[...] = h32[...].astype(bf)
    tok = lax.broadcasted_iota(jnp.int32, (toks, LANES), 0)
    lane = lax.broadcasted_iota(jnp.int32, (toks, LANES), 1)
    position = lax.rem(tok, 2)
    for r in range(rows):
        position = position + jnp.where(lax.div(tok, 2) == r, len_s[r], 0)
    half = lax.rem(lane, 64)
    frequency = jnp.exp(-math.log(500000.0) * (2.0 * half.astype(f32) / 128))
    angle = position.astype(f32) * frequency
    cos_t[...] = jnp.cos(angle)
    sine = jnp.sin(angle)
    sin_t[...] = jnp.where(lane < 64, -sine, sine)
    kn[...] = jnp.zeros_like(kn)
    vn[...] = jnp.zeros_like(vn)
    loads["nk"].wait()
    for r in range(rows):
        kn[2 * r : 2 * r + 2, :] = nk[r].astype(f32)

    for d in order_of(nf):
        zp = turn(zf, nf - d, nf)
        ps, ph = lax.div(zp, nh), lax.rem(zp, nh)
        pa = jnp.where(ps == 0, y, zn)
        pb = jnp.where(ps == 0, zn, y)
        arrived(meta.at[ps, pa, pb, ph], m1_recv.at[d])
        arrived(feats.at[ps, pa, pb, ph], p1_recv.at[d])

    for d in order_of(n_ab):
        for s in range(2):
            mine = (s, a_of[s], b_of[s])
            send(meta.at[mine], meta.at[mine], m2_send.at[s, d], m2_recv.at[s, d], b_peer[s](d))
            send(feats.at[mine], feats.at[mine], p2_send.at[s, d], p2_recv.at[s, d], b_peer[s](d))

    for name in ("wq", "wv"):
        loads[name].wait()
    base[:, :q_w] = jnp.dot(h16[...], wq[...], preferred_element_type=f32)

    for d in order_of(n_ab):
        for s in range(2):
            got = (s, a_of[s], turn(b_of[s], n_ab - d, n_ab))
            arrived(meta.at[got], m2_recv.at[s, d])
            arrived(feats.at[got], p2_recv.at[s, d])

    for d in order_of(n_ab):
        for s in range(2):
            mine = (s, a_of[s])
            send(meta.at[mine], meta.at[mine], m3_send.at[s, d], m3_recv.at[s, d], a_peer[s](d))
            send(feats.at[mine], feats.at[mine], p3_send.at[s, d], p3_recv.at[s, d], a_peer[s](d))

    half_toks = n_ab * nh * toks
    chunk = 2 * half_toks
    piece = chunk // nt

    def products(d):
        if d:
            for s in range(2):
                got = (s, turn(a_of[s], d, n_ab))
                arrived(meta.at[got], m3_recv.at[s, n_ab - d])
                arrived(feats.at[got], p3_recv.at[s, n_ab - d])
        else:
            for k in range(slots):
                loads[f"qd{k}"].wait()
                loads[f"vd{k}"].wait()
        for s in range(2):
            a = turn(a_of[s], d, n_ab)
            x = feats[s, a].reshape(half_toks, part)
            prod = lax.dot_general(
                x, down[...], (((1,), (1,)), ((), ())), preferred_element_type=f32
            )
            codes = meta[s, a].reshape(n_ab * nh, 1, LANES).astype(f32)
            codes = jnp.broadcast_to(codes, (n_ab * nh, toks, LANES))
            lane3 = lax.broadcasted_iota(jnp.int32, codes.shape, 2)
            tok3 = lax.broadcasted_iota(jnp.int32, codes.shape, 1)
            codes = jnp.where(lane3 == lax.div(tok3, 2), codes, 0.0)
            codes = jnp.sum(codes, -1, keepdims=True).reshape(half_toks, 1)
            codes = jnp.broadcast_to(codes, (half_toks, LANES)).astype(jnp.int32)
            rank = lax.rem(codes, 256)
            slot = lax.div(codes, 256)
            place = slot - wide * slots
            locs[d, s] = place
            total = jnp.zeros((half_toks, LANES), f32)
            for k in range(slots):
                total = jnp.where(place == k, prod[:, k * LANES : (k + 1) * LANES], total)
            col = lax.rem(lax.broadcasted_iota(jnp.int32, total.shape, 1), rank_w)
            total = jnp.where(col < rank, total, 0.0)
            n = nt // 2
            mixed[d, s * n : (s + 1) * n] = total.reshape(n, piece, LANES)
        for e in range(1, nt):
            send(
                mixed.at[d, turn(tp, e, nt)],
                arrive_p.at[d, e],
                rs_send.at[d, e],
                rs_recv.at[d, e],
                t_peer(e),
            )

    def reduce(d):
        total = mixed[d, tp]
        for e in range(1, nt):
            arrived(arrive_p.at[d, e], rs_recv.at[d, e])
            total = total + arrive_p[d, e]
        red[d, tp] = total.astype(bf)
        for e in range(1, nt):
            send(red.at[d, tp], red.at[d, tp], ag_send.at[d, e], ag_recv.at[d, e], t_peer(e))

    def expand(d):
        if d == 0:
            for k in range(slots):
                loads[f"qu{k}"].wait()
                loads[f"vu{k}"].wait()
        for e in range(1, nt):
            arrived(red.at[d, turn(tp, nt - e, nt)], ag_recv.at[d, e])
        n = nt // 2
        for s in range(2):
            shrunk = red[d, s * n : (s + 1) * n].reshape(half_toks, LANES).astype(f32)
            place = locs[d, s]
            spread = jnp.concatenate(
                [jnp.where(place == k, shrunk, 0.0).astype(bf) for k in range(slots)], 1
            )
            dq = jnp.dot(spread, upq[...], preferred_element_type=f32).astype(bf)
            dv = jnp.dot(spread, upv[...], preferred_element_type=f32).astype(bf)
            delta[d, s, :, :, :, :q_w] = dq.reshape(n_ab, nh, toks, q_w)
            delta[d, s, :, :, :, q_w:] = dv.reshape(n_ab, nh, toks, v_w)
            if d:
                send(delta.at[d, s], r1.at[s, d], d1_send.at[s, d], d1_recv.at[s, d], a_peer[s](d))

    order = [0] + order_of(n_ab)
    products(order[0])
    base[:, q_w:] = jnp.dot(h16[...], wv[...], preferred_element_type=f32)
    reduce(order[0])
    for i in range(1, len(order)):
        products(order[i])
        expand(order[i - 1])
        reduce(order[i])
    expand(order[-1])

    for s in range(2):
        total = delta[0, s].astype(f32)
        for d in order_of(n_ab):
            arrived(r1.at[s, d], d1_recv.at[s, d])
            total = total + r1[s, d].astype(f32)
        s1[s] = total.astype(bf)
        for d in order_of(n_ab):
            send(
                s1.at[s, turn(b_of[s], d, n_ab)],
                r2.at[s, d],
                d2_send.at[s, d],
                d2_recv.at[s, d],
                b_peer[s](d),
            )
    for s in range(2):
        total = s1[s, b_of[s]].astype(f32)
        for d in order_of(n_ab):
            arrived(r2.at[s, d], d2_recv.at[s, d])
            total = total + r2[s, d].astype(f32)
        s2[s * nh : (s + 1) * nh] = total.astype(bf)
    for d in order_of(nf):
        send(s2.at[turn(zf, d, nf)], r3.at[d], d3_send.at[d], d3_recv.at[d], f_peer(d))
    loads["kc"].wait()
    loads["vc"].wait()
    total = s2[zf].astype(f32)
    for d in order_of(nf):
        arrived(r3.at[d], d3_recv.at[d])
        total = total + r3[d].astype(f32)

    full = base[...] + total
    fresh = full[:, q_w:].astype(bf).astype(f32)
    vn[:toks, :] = fresh
    for r in range(rows):
        new_values[r] = fresh[2 * r : 2 * r + 2].astype(bf)
    heads = q_w // LANES
    turned = []
    for h in range(heads):
        x = full[:, h * LANES : (h + 1) * LANES]
        turned.append(x * cos_t[...] + pltpu.roll(x, 64, 1) * sin_t[...])
    queries = jnp.concatenate(turned, 0).astype(bf)
    many = heads * toks
    inv_root = 1.0 / math.sqrt(LANES)
    row_id = lax.broadcasted_iota(jnp.int32, (many, cache), 0)
    row_of = lax.div(lax.rem(row_id, toks), 2)
    spot = lax.broadcasted_iota(jnp.int32, (many, cache), 1)
    contract = (((1,), (1,)), ((), ()))
    scores = jnp.zeros((many, cache), f32)
    length = jnp.zeros((many, cache), jnp.int32)
    for r in range(rows):
        one = lax.dot_general(queries, kv[r, 0], contract, preferred_element_type=f32)
        scores = jnp.where(row_of == r, one, scores)
        length = jnp.where(row_of == r, len_s[r], length)
    scores = jnp.where(spot < length, scores * inv_root, -jnp.inf)
    fresh_scores = (
        lax.dot_general(queries, kn[...].astype(bf), contract, preferred_element_type=f32)
        * inv_root
    )
    row_n = lax.rem(lax.broadcasted_iota(jnp.int32, fresh_scores.shape, 0), toks)
    col_n = lax.broadcasted_iota(jnp.int32, fresh_scores.shape, 1)
    seen = (lax.div(row_n, 2) == lax.div(col_n, 2)) & (lax.rem(col_n, 2) <= lax.rem(row_n, 2))
    fresh_scores = jnp.where(seen, fresh_scores, -jnp.inf)
    largest = jnp.maximum(
        jnp.max(scores, -1, keepdims=True), jnp.max(fresh_scores, -1, keepdims=True)
    )
    old_weight = jnp.exp(scores - largest)
    new_weight = jnp.exp(fresh_scores - largest)
    denominator = jnp.sum(old_weight, -1, keepdims=True) + jnp.sum(new_weight, -1, keepdims=True)
    old_prob = old_weight / denominator
    new_prob = (new_weight / denominator).astype(bf)
    result = jnp.dot(new_prob, vn[...].astype(bf), preferred_element_type=f32)
    for r in range(rows):
        weights = jnp.where(row_of == r, old_prob, 0.0).astype(bf)
        result = result + jnp.dot(weights, vv[r, 0], preferred_element_type=f32)
    for r in range(rows):
        for h in range(heads):
            at = h * toks + 2 * r
            attended[r, :, h * LANES : (h + 1) * LANES] = result[at : at + 2].astype(bf)
    for c in sends:
        c.wait_send()


def local(dims, *args):
    (hidden, new_keys, key_cache, value_cache, cache_len, adapter_id, adapter_slot, adapter_rank,
     q_weight, v_weight, q_down, v_down, q_up, v_up) = args
    ny, nn, nf, nt = dims
    nh = nf // 2
    rows, _, width = hidden.shape
    toks = rows * 2
    part = width // nt
    slots, rank_w, q_w = q_up.shape
    v_w = v_up.shape[2]
    all_w = q_w + v_w
    piece = 2 * ny * nh * toks // nt
    half_toks = ny * nh * toks
    bf, f32, i32 = jnp.bfloat16, jnp.float32, jnp.int32
    V = pltpu.VMEM
    dma = pltpu.SemaphoreType.DMA
    q_down = jnp.swapaxes(q_down, 1, 2)
    v_down = jnp.swapaxes(v_down, 1, 2)
    scratch = [
        V((rows, 2, width), bf),
        V((toks, width), f32),
        V((toks, width), bf),
        V(key_cache.shape, bf),
        V(value_cache.shape, bf),
        V(new_keys.shape, bf),
        pltpu.SMEM(cache_len.shape, i32),
        pltpu.SMEM(adapter_id.shape, i32),
        pltpu.SMEM(adapter_slot.shape, i32),
        pltpu.SMEM(adapter_rank.shape, i32),
        V(q_weight.shape, bf),
        V(v_weight.shape, bf),
        V((slots * 2 * rank_w, part), bf),
        V((slots * 2 * rank_w, q_w), bf),
        V((slots * 2 * rank_w, v_w), bf),
        V((2, ny, ny, nh, toks, part), bf),
        V((2, ny, ny, nh, 1, LANES), i32),
        V((ny, 2, half_toks, LANES), i32),
        V((ny, nt, piece, LANES), f32),
        V((ny, nt, piece, LANES), f32),
        V((ny, nt, piece, LANES), bf),
        V((ny, 2, ny, nh, toks, all_w), bf),
        V((2, ny, ny, nh, toks, all_w), bf),
        V((2, ny, nh, toks, all_w), bf),
        V((2, ny, nh, toks, all_w), bf),
        V((nf, toks, all_w), bf),
        V((nf, toks, all_w), bf),
        V((toks, all_w), f32),
        V((toks, LANES), f32),
        V((toks, LANES), f32),
        V((LANES, LANES), f32),
        V((LANES, LANES), f32),
        dma((8 + 4 * slots + 2,)),
    ]
    for shape in ((nf,), (nf,), (2, ny), (2, ny), (2, ny), (2, ny), (ny, nt), (ny, nt),
                  (2, ny), (2, ny), (nf,)):
        scratch += [dma(shape), dma(shape)]
    any_space = pl.BlockSpec(memory_space=pl.ANY)
    vmem = pl.BlockSpec(memory_space=pltpu.VMEM)
    return tuple(
        pl.pallas_call(
            functools.partial(kernel, dims),
            out_shape=(
                jax.ShapeDtypeStruct((rows, 2, q_w), bf),
                jax.ShapeDtypeStruct((rows, 2, v_w), bf),
            ),
            in_specs=[any_space] * 14,
            out_specs=(vmem, vmem),
            scratch_shapes=scratch,
            compiler_params=pltpu.CompilerParams(
                collective_id=0, has_side_effects=True, vmem_limit_bytes=56 * 1024 * 1024
            ),
        )(hidden, new_keys, key_cache, value_cache, cache_len, adapter_id, adapter_slot,
          adapter_rank, q_weight, v_weight, q_down, v_down, q_up, v_up)
    )


def solution(mesh):
    dims = factors(mesh.shape["wide"]) + (mesh.shape["tp"],)
    return jax.shard_map(
        functools.partial(local, dims),
        mesh=mesh,
        in_specs=(
            P("wide", None, None),
            P("wide", None, "tp"),
            P("wide", "tp", None, None),
            P("wide", "tp", None, None),
            P("wide"),
            P("wide"),
            P(),
            P(),
            P(None, "tp"),
            P(None, "tp"),
            P("wide", "tp", None),
            P("wide", "tp", None),
            P("wide", None, "tp"),
            P("wide", None, "tp"),
        ),
        out_specs=(P("wide", None, "tp"), P("wide", None, "tp")),
        check_vma=False,
    )
```

```python
import functools
import math

import jax
import jax.numpy as jnp
from jax import lax
from jax.experimental import pallas as pl
from jax.experimental.pallas import tpu as pltpu
from jax.sharding import PartitionSpec as P

MESH = pl.DeviceIdType.MESH
LANES = 128


def factors(wide):
    return (4, 4, wide // 16) if wide >= 32 else (2, 2, wide // 4)


def order_of(n):
    near = [d for d in (1, n - 1) if d < n]
    return list(dict.fromkeys(near + list(range(1, n))))


def kernel(
    dims,
    hidden,
    new_keys,
    key_cache,
    value_cache,
    cache_len,
    adapter_id,
    adapter_slot,
    adapter_rank,
    q_weight,
    v_weight,
    q_down,
    v_down,
    q_up,
    v_up,
    attended,
    new_values,
    hid,
    hid_part,
    h32,
    h16,
    kv,
    vv,
    nk,
    len_s,
    id_s,
    slot_s,
    rank_s,
    wq,
    wv,
    down,
    upq,
    upv,
    feats,
    mixed,
    arrive_p,
    red,
    delta,
    back,
    far_out,
    far_in,
    base,
    cos_t,
    sin_t,
    kn,
    vn,
    local_sem,
    f_send,
    f_recv,
    n_send,
    n_recv,
    rs_send,
    rs_recv,
    ag_send,
    ag_recv,
    b_send,
    b_recv,
    r_send,
    r_recv,
):
    ny, nn, nf, nt = dims
    near = ny * nn
    rows, _, width = hidden.shape
    toks = rows * 2
    part = width // nt
    slots = q_up.shape[0]
    rank_w = q_up.shape[1]
    q_w = q_up.shape[2]
    v_w = v_up.shape[2]
    cache = key_cache.shape[2]
    adapters = adapter_slot.shape[0]
    chunk = near * toks
    piece = chunk // nt
    bf, f32 = jnp.bfloat16, jnp.float32

    wide = lax.axis_index("wide")
    tp = lax.axis_index("tp")
    y = lax.div(wide, nf * nn)
    z = lax.rem(wide, nf * nn)
    zf = lax.div(z, nn)
    zn = lax.rem(z, nn)

    def turn(i, d, n):
        return lax.rem(i + d, n)

    def f_peer(d):
        return (y * (nf * nn) + turn(zf, d, nf) * nn + zn, tp)

    def n_peer(e):
        return (turn(y, e // nn, ny) * (nf * nn) + zf * nn + turn(zn, e % nn, nn), tp)

    def t_peer(e):
        return (wide, turn(tp, e, nt))

    def n_back(e):
        return (-(e // nn) % ny) * nn + (-(e % nn)) % nn

    loads = {}

    def load(name, src, dst, i):
        c = pltpu.make_async_copy(src, dst, local_sem.at[i])
        c.start()
        loads[name] = c

    def loaded(name):
        loads.pop(name).wait()

    col = pl.multiple_of(tp * part, part)
    load("hp", hidden.at[:, :, pl.ds(col, part)], hid_part, 0)
    load("id", adapter_id, id_s, 1)
    load("slot", adapter_slot, slot_s, 2)
    load("rank", adapter_rank, rank_s, 3)

    barrier = pltpu.get_barrier_semaphore()
    peers = (
        [f_peer(d) for d in order_of(nf)[::-1]]
        + [n_peer(e) for e in range(1, near)]
        + [t_peer(e) for e in range(1, nt)]
    )
    for p in peers:
        pl.semaphore_signal(barrier, inc=1, device_id=p, device_id_type=MESH)

    for name in ("id", "slot", "rank"):
        loaded(name)
    tok = lax.broadcasted_iota(jnp.int32, (toks, LANES), 0)
    lane = lax.broadcasted_iota(jnp.int32, (toks, LANES), 1)
    code = jnp.zeros((toks, LANES), jnp.int32)
    for r in range(rows):
        ident = id_s[r]
        mine = jnp.where(lax.rem(lane, rank_w) < rank_s[ident], slot_s[ident], adapters)
        code = jnp.where(lax.div(tok, 2) == r, mine, code)
    feats[0, 0, :, part:] = code.astype(f32).astype(bf)
    loaded("hp")
    for r in range(rows):
        h32[2 * r : 2 * r + 2, :part] = hid_part[r].astype(f32)
    feats[0, 0, :, :part] = h32[:, :part].astype(bf)

    def send(src, dst, ssem, rsem, peer):
        pltpu.make_async_remote_copy(
            src_ref=src,
            dst_ref=dst,
            send_sem=ssem,
            recv_sem=rsem,
            device_id=peer,
            device_id_type=MESH,
        ).start()

    def passed(ref, sem):
        pltpu.make_async_copy(ref, ref, sem).wait()

    pl.semaphore_wait(barrier, len(peers))

    for d in order_of(nf)[::-1]:
        send(feats.at[0, 0], feats.at[nf - d, 0], f_send.at[d], f_recv.at[nf - d], f_peer(d))

    def spread_near(d):
        if d:
            passed(feats.at[d, 0], f_recv.at[d])
        for e in range(1, near):
            send(feats.at[d, 0], feats.at[d, n_back(e)], n_send.at[d], n_recv.at[d], n_peer(e))

    def products(d):
        passed(feats.at[d, pl.ds(1, near - 1)], n_recv.at[d])
        x = feats[d, :, :, :part].reshape(chunk, part)
        place = feats[d, :, :, part:].reshape(chunk, LANES).astype(f32)
        place = place - (wide * slots).astype(f32)
        prod = lax.dot_general(x, down[...], (((1,), (1,)), ((), ())), preferred_element_type=f32)
        total = jnp.zeros((chunk, LANES), f32)
        for k in range(slots):
            total = jnp.where(place == float(k), prod[:, k * LANES : (k + 1) * LANES], total)
        mixed[d] = total.reshape(nt, piece, LANES)
        for e in range(1, nt):
            send(
                mixed.at[d, turn(tp, e, nt)],
                arrive_p.at[d, nt - e],
                rs_send.at[d],
                rs_recv.at[d],
                t_peer(e),
            )

    def reduce(d):
        passed(arrive_p.at[d, pl.ds(1, nt - 1)], rs_recv.at[d])
        total = mixed[d, tp]
        for e in range(1, nt):
            total = total + arrive_p[d, e]
        red[d, 0] = total.astype(bf)
        for e in range(1, nt):
            send(red.at[d, 0], red.at[d, nt - e], ag_send.at[d], ag_recv.at[d], t_peer(e))

    def expand(d):
        passed(red.at[d, pl.ds(1, nt - 1)], ag_recv.at[d])
        shrunk = jnp.concatenate(
            [red[d, turn(nt - tp, p, nt)].astype(f32) for p in range(nt)], 0
        )
        place = feats[d, :, :, part:].reshape(chunk, LANES).astype(f32)
        place = place - (wide * slots).astype(f32)
        spread = jnp.concatenate(
            [jnp.where(place == float(k), shrunk, 0.0).astype(bf) for k in range(slots)], 1
        )
        dq = jnp.dot(spread, upq[...], preferred_element_type=f32).astype(bf)
        dv = jnp.dot(spread, upv[...], preferred_element_type=f32).astype(bf)
        delta[d, :, :, :q_w] = dq.reshape(near, toks, q_w)
        delta[d, :, :, q_w:] = dv.reshape(near, toks, v_w)
        for e in range(1, near):
            send(delta.at[d, e], back.at[d, n_back(e)], b_send.at[d], b_recv.at[d], n_peer(e))

    def gather_back(d):
        passed(back.at[d, pl.ds(1, near - 1)], b_recv.at[d])
        total = delta[d, 0].astype(f32) + jnp.sum(back[d, 1:].astype(f32), 0)
        far_out[d] = total.astype(bf)
        if d:
            send(far_out.at[d], far_in.at[nf - d], r_send.at[d], r_recv.at[nf - d], f_peer(d))

    spread_near(0)

    load("hid", hidden, hid, 0)
    load("len", cache_len, len_s, 4)
    load("nk", new_keys, nk, 5)
    for k in range(slots):
        row = k * 2 * rank_w
        load(f"qd{k}", q_down.at[k], down.at[pl.ds(row, rank_w)], 8 + 4 * k)
        load(f"vd{k}", v_down.at[k], down.at[pl.ds(row + rank_w, rank_w)], 9 + 4 * k)
    load("wq", q_weight, wq, 6)
    load("wv", v_weight, wv, 7)
    upq[...] = jnp.zeros_like(upq)
    upv[...] = jnp.zeros_like(upv)
    for k in range(slots):
        row = k * 2 * rank_w
        load(f"qu{k}", q_up.at[k], upq.at[pl.ds(row, rank_w)], 10 + 4 * k)
        load(f"vu{k}", v_up.at[k], upv.at[pl.ds(row + rank_w, rank_w)], 11 + 4 * k)
    n0 = 8 + 4 * slots
    load("kc", key_cache, kv, n0)
    load("vc", value_cache, vv, n0 + 1)
    loaded("hid")
    for r in range(rows):
        h32[2 * r : 2 * r + 2, :] = hid[r].astype(f32)
    h16[...] = h32[...].astype(bf)
    loaded("len")
    position = lax.rem(tok, 2)
    for r in range(rows):
        position = position + jnp.where(lax.div(tok, 2) == r, len_s[r], 0)
    half = lax.rem(lane, 64)
    frequency = jnp.exp(-math.log(500000.0) * (2.0 * half.astype(f32) / 128))
    angle = position.astype(f32) * frequency
    cos_t[...] = jnp.cos(angle)
    sine = jnp.sin(angle)
    sin_t[...] = jnp.where(lane < 64, -sine, sine)
    kn[...] = jnp.zeros_like(kn)
    vn[...] = jnp.zeros_like(vn)
    loaded("nk")
    for r in range(rows):
        kn[2 * r : 2 * r + 2, :] = nk[r].astype(f32)

    order = order_of(nf)
    for d in order[:-1]:
        spread_near(d)
    for k in range(slots):
        loaded(f"qd{k}")
        loaded(f"vd{k}")
    products(0)
    spread_near(order[-1])
    for name in ("wq", "wv"):
        loaded(name)
    base[:, :q_w] = jnp.dot(h16[...], wq[...], preferred_element_type=f32)
    reduce(0)
    for d in order:
        products(d)
    for k in range(slots):
        loaded(f"qu{k}")
        loaded(f"vu{k}")
    expand(0)
    for d in order:
        reduce(d)
    base[:, q_w:] = jnp.dot(h16[...], wv[...], preferred_element_type=f32)
    gather_back(0)
    for d in order:
        expand(d)
    loaded("kc")
    loaded("vc")
    for d in order:
        gather_back(d)
    for d in range(nf):
        if d:
            passed(feats.at[0, 0], f_send.at[d])
        passed(feats.at[d, pl.ds(1, near - 1)], n_send.at[d])
        passed(arrive_p.at[d, pl.ds(1, nt - 1)], rs_send.at[d])
        passed(red.at[d, pl.ds(1, nt - 1)], ag_send.at[d])
        passed(back.at[d, pl.ds(1, near - 1)], b_send.at[d])
    total = far_out[0].astype(f32)
    for d in order:
        passed(far_in.at[d], r_recv.at[d])
        total = total + far_in[d].astype(f32)

    full = base[...] + total
    fresh = full[:, q_w:].astype(bf).astype(f32)
    vn[:toks, :] = fresh
    for r in range(rows):
        new_values[r] = fresh[2 * r : 2 * r + 2].astype(bf)
    heads = q_w // LANES
    turned = []
    for h in range(heads):
        x = full[:, h * LANES : (h + 1) * LANES]
        turned.append(x * cos_t[...] + pltpu.roll(x, 64, 1) * sin_t[...])
    queries = jnp.concatenate(turned, 0).astype(bf)
    many = heads * toks
    inv_root = 1.0 / math.sqrt(LANES)
    row_id = lax.broadcasted_iota(jnp.int32, (many, cache), 0)
    row_of = lax.div(lax.rem(row_id, toks), 2)
    spot = lax.broadcasted_iota(jnp.int32, (many, cache), 1)
    contract = (((1,), (1,)), ((), ()))
    scores = jnp.zeros((many, cache), f32)
    length = jnp.zeros((many, cache), jnp.int32)
    for r in range(rows):
        one = lax.dot_general(queries, kv[r, 0], contract, preferred_element_type=f32)
        scores = jnp.where(row_of == r, one, scores)
        length = jnp.where(row_of == r, len_s[r], length)
    scores = jnp.where(spot < length, scores * inv_root, -jnp.inf)
    fresh_scores = (
        lax.dot_general(queries, kn[...].astype(bf), contract, preferred_element_type=f32)
        * inv_root
    )
    row_n = lax.rem(lax.broadcasted_iota(jnp.int32, fresh_scores.shape, 0), toks)
    col_n = lax.broadcasted_iota(jnp.int32, fresh_scores.shape, 1)
    seen = (lax.div(row_n, 2) == lax.div(col_n, 2)) & (lax.rem(col_n, 2) <= lax.rem(row_n, 2))
    fresh_scores = jnp.where(seen, fresh_scores, -jnp.inf)
    largest = jnp.maximum(
        jnp.max(scores, -1, keepdims=True), jnp.max(fresh_scores, -1, keepdims=True)
    )
    old_weight = jnp.exp(scores - largest)
    new_weight = jnp.exp(fresh_scores - largest)
    denominator = jnp.sum(old_weight, -1, keepdims=True) + jnp.sum(new_weight, -1, keepdims=True)
    old_prob = old_weight / denominator
    new_prob = (new_weight / denominator).astype(bf)
    result = jnp.dot(new_prob, vn[...].astype(bf), preferred_element_type=f32)
    for r in range(rows):
        weights = jnp.where(row_of == r, old_prob, 0.0).astype(bf)
        result = result + jnp.dot(weights, vv[r, 0], preferred_element_type=f32)
    for r in range(rows):
        for h in range(heads):
            at = h * toks + 2 * r
            attended[r, :, h * LANES : (h + 1) * LANES] = result[at : at + 2].astype(bf)
    for d in order:
        passed(far_out.at[d], r_send.at[d])


def local(dims, *args):
    (hidden, new_keys, key_cache, value_cache, cache_len, adapter_id, adapter_slot, adapter_rank,
     q_weight, v_weight, q_down, v_down, q_up, v_up) = args
    ny, nn, nf, nt = dims
    near = ny * nn
    rows, _, width = hidden.shape
    toks = rows * 2
    part = width // nt
    slots, rank_w, q_w = q_up.shape
    v_w = v_up.shape[2]
    all_w = q_w + v_w
    piece = near * toks // nt
    bf, f32, i32 = jnp.bfloat16, jnp.float32, jnp.int32
    V = pltpu.VMEM
    dma = pltpu.SemaphoreType.DMA
    q_down = jnp.swapaxes(q_down, 1, 2)
    v_down = jnp.swapaxes(v_down, 1, 2)
    scratch = [
        V((rows, 2, width), bf),
        V((rows, 2, part), bf),
        V((toks, width), f32),
        V((toks, width), bf),
        V(key_cache.shape, bf),
        V(value_cache.shape, bf),
        V(new_keys.shape, bf),
        pltpu.SMEM(cache_len.shape, i32),
        pltpu.SMEM(adapter_id.shape, i32),
        pltpu.SMEM(adapter_slot.shape, i32),
        pltpu.SMEM(adapter_rank.shape, i32),
        V(q_weight.shape, bf),
        V(v_weight.shape, bf),
        V((slots * 2 * rank_w, part), bf),
        V((slots * 2 * rank_w, q_w), bf),
        V((slots * 2 * rank_w, v_w), bf),
        V((nf, near, toks, part + LANES), bf),
        V((nf, nt, piece, LANES), f32),
        V((nf, nt, piece, LANES), f32),
        V((nf, nt, piece, LANES), bf),
        V((nf, near, toks, all_w), bf),
        V((nf, near, toks, all_w), bf),
        V((nf, toks, all_w), bf),
        V((nf, toks, all_w), bf),
        V((toks, all_w), f32),
        V((toks, LANES), f32),
        V((toks, LANES), f32),
        V((LANES, LANES), f32),
        V((LANES, LANES), f32),
        dma((8 + 4 * slots + 2,)),
    ]
    scratch += [dma((nf,)) for _ in range(12)]
    any_space = pl.BlockSpec(memory_space=pl.ANY)
    vmem = pl.BlockSpec(memory_space=pltpu.VMEM)
    return tuple(
        pl.pallas_call(
            functools.partial(kernel, dims),
            out_shape=(
                jax.ShapeDtypeStruct((rows, 2, q_w), bf),
                jax.ShapeDtypeStruct((rows, 2, v_w), bf),
            ),
            in_specs=[any_space] * 14,
            out_specs=(vmem, vmem),
            scratch_shapes=scratch,
            compiler_params=pltpu.CompilerParams(
                collective_id=0, has_side_effects=True, vmem_limit_bytes=56 * 1024 * 1024
            ),
        )(hidden, new_keys, key_cache, value_cache, cache_len, adapter_id, adapter_slot,
          adapter_rank, q_weight, v_weight, q_down, v_down, q_up, v_up)
    )


def solution(mesh):
    dims = factors(mesh.shape["wide"]) + (mesh.shape["tp"],)
    return jax.shard_map(
        functools.partial(local, dims),
        mesh=mesh,
        in_specs=(
            P("wide", None, None),
            P("wide", None, "tp"),
            P("wide", "tp", None, None),
            P("wide", "tp", None, None),
            P("wide"),
            P("wide"),
            P(),
            P(),
            P(None, "tp"),
            P(None, "tp"),
            P("wide", "tp", None),
            P("wide", "tp", None),
            P("wide", None, "tp"),
            P("wide", None, "tp"),
        ),
        out_specs=(P("wide", None, "tp"), P("wide", None, "tp")),
        check_vma=False,
    )
```

```python
import functools
import math

import jax
import jax.numpy as jnp
from jax import lax
from jax.experimental import pallas as pl
from jax.experimental.pallas import tpu as pltpu
from jax.sharding import PartitionSpec as P

MESH = pl.DeviceIdType.MESH
LANES = 128


def factors(wide):
    return (4, 4, wide // 16) if wide >= 32 else (2, 2, wide // 4)


def order_of(n):
    near = [d for d in (1, n - 1) if d < n]
    return list(dict.fromkeys(near + list(range(1, n))))


def kernel(
    dims,
    hidden,
    new_keys,
    key_cache,
    value_cache,
    cache_len,
    adapter_id,
    adapter_slot,
    adapter_rank,
    q_weight,
    v_weight,
    q_down,
    v_down,
    q_up,
    v_up,
    attended,
    new_values,
    hid,
    hid_part,
    h32,
    h16,
    kv,
    vv,
    nk,
    len_s,
    id_s,
    slot_s,
    rank_s,
    wq,
    wv,
    down,
    upq,
    upv,
    feats,
    mixed,
    arrive_p,
    red,
    delta,
    back,
    far_out,
    far_in,
    base,
    cos_t,
    sin_t,
    kn,
    vn,
    local_sem,
    f_send,
    f_recv,
    n_send,
    n_recv,
    rs_send,
    rs_recv,
    ag_send,
    ag_recv,
    b_send,
    b_recv,
    r_send,
    r_recv,
):
    ny, nn, nf, nt = dims
    near = ny * nn
    rows, _, width = hidden.shape
    toks = rows * 2
    part = width // nt
    slots = q_up.shape[0]
    rank_w = q_up.shape[1]
    q_w = q_up.shape[2]
    v_w = v_up.shape[2]
    cache = key_cache.shape[2]
    adapters = adapter_slot.shape[0]
    chunk = near * toks
    piece = chunk // nt
    bf, f32 = jnp.bfloat16, jnp.float32

    wide = lax.axis_index("wide")
    tp = lax.axis_index("tp")
    nz = nf * nn
    y = lax.div(wide, nz)
    z = lax.rem(wide, nz)

    def turn(i, d, n):
        return lax.rem(i + d, n)

    def f_peer(d):
        return (y * nz + turn(z, d * nn, nz), tp)

    even = lax.rem(z, 2) == 0
    steps = (0, 1, jnp.where(even, 2, nz - 2), nz - 1) if nn == 4 else (0, jnp.where(even, 1, nz - 1))
    homes = tuple(nz - s if i == 2 else s for i, s in enumerate(steps))

    def n_peer(e):
        return (turn(y, e // nn, ny) * nz + turn(z, steps[e % nn], nz), tp)

    def h_peer(e):
        return (turn(y, e // nn, ny) * nz + turn(z, homes[e % nn], nz), tp)

    def t_peer(e):
        return (wide, turn(tp, e, nt))

    def n_back(e):
        return (-(e // nn) % ny) * nn + (-(e % nn)) % nn

    loads = {}

    def load(name, src, dst, i):
        c = pltpu.make_async_copy(src, dst, local_sem.at[i])
        c.start()
        loads[name] = c

    def loaded(name):
        loads.pop(name).wait()

    col = pl.multiple_of(tp * part, part)
    load("hp", hidden.at[:, :, pl.ds(col, part)], hid_part, 0)
    load("id", adapter_id, id_s, 1)
    load("slot", adapter_slot, slot_s, 2)
    load("rank", adapter_rank, rank_s, 3)

    barrier = pltpu.get_barrier_semaphore()
    peers = (
        [f_peer(d) for d in order_of(nf)[::-1]]
        + [n_peer(e) for e in range(1, near)]
        + [h_peer(e) for e in range(1, near) if e % nn == 2]
        + [t_peer(e) for e in range(1, nt)]
    )
    for p in peers:
        pl.semaphore_signal(barrier, inc=1, device_id=p, device_id_type=MESH)

    for name in ("id", "slot", "rank"):
        loaded(name)
    tok = lax.broadcasted_iota(jnp.int32, (toks, LANES), 0)
    lane = lax.broadcasted_iota(jnp.int32, (toks, LANES), 1)
    code = jnp.zeros((toks, LANES), jnp.int32)
    for r in range(rows):
        ident = id_s[r]
        mine = jnp.where(lax.rem(lane, rank_w) < rank_s[ident], slot_s[ident], adapters)
        code = jnp.where(lax.div(tok, 2) == r, mine, code)
    feats[0, 0, :, part:] = code.astype(f32).astype(bf)
    loaded("hp")
    for r in range(rows):
        h32[2 * r : 2 * r + 2, :part] = hid_part[r].astype(f32)
    feats[0, 0, :, :part] = h32[:, :part].astype(bf)

    def send(src, dst, ssem, rsem, peer):
        pltpu.make_async_remote_copy(
            src_ref=src,
            dst_ref=dst,
            send_sem=ssem,
            recv_sem=rsem,
            device_id=peer,
            device_id_type=MESH,
        ).start()

    def passed(ref, sem):
        pltpu.make_async_copy(ref, ref, sem).wait()

    pl.semaphore_wait(barrier, len(peers))

    for d in order_of(nf)[::-1]:
        send(feats.at[0, 0], feats.at[nf - d, 0], f_send.at[d], f_recv.at[nf - d], f_peer(d))

    def spread_near(d):
        if d:
            passed(feats.at[d, 0], f_recv.at[d])
        for e in range(1, near):
            send(feats.at[d, 0], feats.at[d, n_back(e)], n_send.at[d], n_recv.at[d], n_peer(e))

    def products(d):
        passed(feats.at[d, pl.ds(1, near - 1)], n_recv.at[d])
        x = feats[d, :, :, :part].reshape(chunk, part)
        place = feats[d, :, :, part:].reshape(chunk, LANES).astype(f32)
        place = place - (wide * slots).astype(f32)
        prod = lax.dot_general(x, down[...], (((1,), (1,)), ((), ())), preferred_element_type=f32)
        total = jnp.zeros((chunk, LANES), f32)
        for k in range(slots):
            total = jnp.where(place == float(k), prod[:, k * LANES : (k + 1) * LANES], total)
        mixed[d] = total.reshape(nt, piece, LANES)
        for e in range(1, nt):
            send(
                mixed.at[d, turn(tp, e, nt)],
                arrive_p.at[d, nt - e],
                rs_send.at[d],
                rs_recv.at[d],
                t_peer(e),
            )

    def reduce(d):
        passed(arrive_p.at[d, pl.ds(1, nt - 1)], rs_recv.at[d])
        total = mixed[d, tp]
        for e in range(1, nt):
            total = total + arrive_p[d, e]
        red[d, 0] = total.astype(bf)
        for e in range(1, nt):
            send(red.at[d, 0], red.at[d, nt - e], ag_send.at[d], ag_recv.at[d], t_peer(e))

    def expand(d):
        passed(red.at[d, pl.ds(1, nt - 1)], ag_recv.at[d])
        shrunk = jnp.concatenate(
            [red[d, turn(nt - tp, p, nt)].astype(f32) for p in range(nt)], 0
        )
        place = feats[d, :, :, part:].reshape(chunk, LANES).astype(f32)
        place = place - (wide * slots).astype(f32)
        spread = jnp.concatenate(
            [jnp.where(place == float(k), shrunk, 0.0).astype(bf) for k in range(slots)], 1
        )
        dq = jnp.dot(spread, upq[...], preferred_element_type=f32).astype(bf)
        dv = jnp.dot(spread, upv[...], preferred_element_type=f32).astype(bf)
        delta[d, :, :, :q_w] = dq.reshape(near, toks, q_w)
        delta[d, :, :, q_w:] = dv.reshape(near, toks, v_w)
        for e in range(1, near):
            send(delta.at[d, e], back.at[d, n_back(e)], b_send.at[d], b_recv.at[d], h_peer(e))

    def gather_back(d):
        passed(back.at[d, pl.ds(1, near - 1)], b_recv.at[d])
        total = delta[d, 0].astype(f32) + jnp.sum(back[d, 1:].astype(f32), 0)
        far_out[d] = total.astype(bf)
        if d:
            send(far_out.at[d], far_in.at[nf - d], r_send.at[d], r_recv.at[nf - d], f_peer(d))

    spread_near(0)

    load("hid", hidden, hid, 0)
    load("len", cache_len, len_s, 4)
    load("nk", new_keys, nk, 5)
    for k in range(slots):
        row = k * 2 * rank_w
        load(f"qd{k}", q_down.at[k], down.at[pl.ds(row, rank_w)], 8 + 4 * k)
        load(f"vd{k}", v_down.at[k], down.at[pl.ds(row + rank_w, rank_w)], 9 + 4 * k)
    load("wq", q_weight, wq, 6)
    load("wv", v_weight, wv, 7)
    upq[...] = jnp.zeros_like(upq)
    upv[...] = jnp.zeros_like(upv)
    for k in range(slots):
        row = k * 2 * rank_w
        load(f"qu{k}", q_up.at[k], upq.at[pl.ds(row, rank_w)], 10 + 4 * k)
        load(f"vu{k}", v_up.at[k], upv.at[pl.ds(row + rank_w, rank_w)], 11 + 4 * k)
    n0 = 8 + 4 * slots
    load("kc", key_cache, kv, n0)
    load("vc", value_cache, vv, n0 + 1)
    loaded("hid")
    for r in range(rows):
        h32[2 * r : 2 * r + 2, :] = hid[r].astype(f32)
    h16[...] = h32[...].astype(bf)
    loaded("len")
    position = lax.rem(tok, 2)
    for r in range(rows):
        position = position + jnp.where(lax.div(tok, 2) == r, len_s[r], 0)
    half = lax.rem(lane, 64)
    frequency = jnp.exp(-math.log(500000.0) * (2.0 * half.astype(f32) / 128))
    angle = position.astype(f32) * frequency
    cos_t[...] = jnp.cos(angle)
    sine = jnp.sin(angle)
    sin_t[...] = jnp.where(lane < 64, -sine, sine)
    kn[...] = jnp.zeros_like(kn)
    vn[...] = jnp.zeros_like(vn)
    loaded("nk")
    for r in range(rows):
        kn[2 * r : 2 * r + 2, :] = nk[r].astype(f32)

    order = order_of(nf)
    for d in order[:-1]:
        spread_near(d)
    for k in range(slots):
        loaded(f"qd{k}")
        loaded(f"vd{k}")
    products(0)
    spread_near(order[-1])
    for name in ("wq", "wv"):
        loaded(name)
    base[:, :q_w] = jnp.dot(h16[...], wq[...], preferred_element_type=f32)
    reduce(0)
    for d in order:
        products(d)
    for k in range(slots):
        loaded(f"qu{k}")
        loaded(f"vu{k}")
    expand(0)
    for d in order:
        reduce(d)
    base[:, q_w:] = jnp.dot(h16[...], wv[...], preferred_element_type=f32)
    gather_back(0)
    for d in order:
        expand(d)
    loaded("kc")
    loaded("vc")
    for d in order:
        gather_back(d)
    for d in range(nf):
        if d:
            passed(feats.at[0, 0], f_send.at[d])
        passed(feats.at[d, pl.ds(1, near - 1)], n_send.at[d])
        passed(arrive_p.at[d, pl.ds(1, nt - 1)], rs_send.at[d])
        passed(red.at[d, pl.ds(1, nt - 1)], ag_send.at[d])
        passed(back.at[d, pl.ds(1, near - 1)], b_send.at[d])
    total = far_out[0].astype(f32)
    for d in order:
        passed(far_in.at[d], r_recv.at[d])
        total = total + far_in[d].astype(f32)

    full = base[...] + total
    fresh = full[:, q_w:].astype(bf).astype(f32)
    vn[:toks, :] = fresh
    for r in range(rows):
        new_values[r] = fresh[2 * r : 2 * r + 2].astype(bf)
    heads = q_w // LANES
    turned = []
    for h in range(heads):
        x = full[:, h * LANES : (h + 1) * LANES]
        turned.append(x * cos_t[...] + pltpu.roll(x, 64, 1) * sin_t[...])
    queries = jnp.concatenate(turned, 0).astype(bf)
    many = heads * toks
    inv_root = 1.0 / math.sqrt(LANES)
    row_id = lax.broadcasted_iota(jnp.int32, (many, cache), 0)
    row_of = lax.div(lax.rem(row_id, toks), 2)
    spot = lax.broadcasted_iota(jnp.int32, (many, cache), 1)
    contract = (((1,), (1,)), ((), ()))
    scores = jnp.zeros((many, cache), f32)
    length = jnp.zeros((many, cache), jnp.int32)
    for r in range(rows):
        one = lax.dot_general(queries, kv[r, 0], contract, preferred_element_type=f32)
        scores = jnp.where(row_of == r, one, scores)
        length = jnp.where(row_of == r, len_s[r], length)
    scores = jnp.where(spot < length, scores * inv_root, -jnp.inf)
    fresh_scores = (
        lax.dot_general(queries, kn[...].astype(bf), contract, preferred_element_type=f32)
        * inv_root
    )
    row_n = lax.rem(lax.broadcasted_iota(jnp.int32, fresh_scores.shape, 0), toks)
    col_n = lax.broadcasted_iota(jnp.int32, fresh_scores.shape, 1)
    seen = (lax.div(row_n, 2) == lax.div(col_n, 2)) & (lax.rem(col_n, 2) <= lax.rem(row_n, 2))
    fresh_scores = jnp.where(seen, fresh_scores, -jnp.inf)
    largest = jnp.maximum(
        jnp.max(scores, -1, keepdims=True), jnp.max(fresh_scores, -1, keepdims=True)
    )
    old_weight = jnp.exp(scores - largest)
    new_weight = jnp.exp(fresh_scores - largest)
    denominator = jnp.sum(old_weight, -1, keepdims=True) + jnp.sum(new_weight, -1, keepdims=True)
    old_prob = old_weight / denominator
    new_prob = (new_weight / denominator).astype(bf)
    result = jnp.dot(new_prob, vn[...].astype(bf), preferred_element_type=f32)
    for r in range(rows):
        weights = jnp.where(row_of == r, old_prob, 0.0).astype(bf)
        result = result + jnp.dot(weights, vv[r, 0], preferred_element_type=f32)
    for r in range(rows):
        for h in range(heads):
            at = h * toks + 2 * r
            attended[r, :, h * LANES : (h + 1) * LANES] = result[at : at + 2].astype(bf)
    for d in order:
        passed(far_out.at[d], r_send.at[d])


def local(dims, *args):
    (hidden, new_keys, key_cache, value_cache, cache_len, adapter_id, adapter_slot, adapter_rank,
     q_weight, v_weight, q_down, v_down, q_up, v_up) = args
    ny, nn, nf, nt = dims
    near = ny * nn
    rows, _, width = hidden.shape
    toks = rows * 2
    part = width // nt
    slots, rank_w, q_w = q_up.shape
    v_w = v_up.shape[2]
    all_w = q_w + v_w
    piece = near * toks // nt
    bf, f32, i32 = jnp.bfloat16, jnp.float32, jnp.int32
    V = pltpu.VMEM
    dma = pltpu.SemaphoreType.DMA
    q_down = jnp.swapaxes(q_down, 1, 2)
    v_down = jnp.swapaxes(v_down, 1, 2)
    scratch = [
        V((rows, 2, width), bf),
        V((rows, 2, part), bf),
        V((toks, width), f32),
        V((toks, width), bf),
        V(key_cache.shape, bf),
        V(value_cache.shape, bf),
        V(new_keys.shape, bf),
        pltpu.SMEM(cache_len.shape, i32),
        pltpu.SMEM(adapter_id.shape, i32),
        pltpu.SMEM(adapter_slot.shape, i32),
        pltpu.SMEM(adapter_rank.shape, i32),
        V(q_weight.shape, bf),
        V(v_weight.shape, bf),
        V((slots * 2 * rank_w, part), bf),
        V((slots * 2 * rank_w, q_w), bf),
        V((slots * 2 * rank_w, v_w), bf),
        V((nf, near, toks, part + LANES), bf),
        V((nf, nt, piece, LANES), f32),
        V((nf, nt, piece, LANES), f32),
        V((nf, nt, piece, LANES), bf),
        V((nf, near, toks, all_w), bf),
        V((nf, near, toks, all_w), bf),
        V((nf, toks, all_w), bf),
        V((nf, toks, all_w), bf),
        V((toks, all_w), f32),
        V((toks, LANES), f32),
        V((toks, LANES), f32),
        V((LANES, LANES), f32),
        V((LANES, LANES), f32),
        dma((8 + 4 * slots + 2,)),
    ]
    scratch += [dma((nf,)) for _ in range(12)]
    any_space = pl.BlockSpec(memory_space=pl.ANY)
    vmem = pl.BlockSpec(memory_space=pltpu.VMEM)
    return tuple(
        pl.pallas_call(
            functools.partial(kernel, dims),
            out_shape=(
                jax.ShapeDtypeStruct((rows, 2, q_w), bf),
                jax.ShapeDtypeStruct((rows, 2, v_w), bf),
            ),
            in_specs=[any_space] * 14,
            out_specs=(vmem, vmem),
            scratch_shapes=scratch,
            compiler_params=pltpu.CompilerParams(
                collective_id=0, has_side_effects=True, vmem_limit_bytes=56 * 1024 * 1024
            ),
        )(hidden, new_keys, key_cache, value_cache, cache_len, adapter_id, adapter_slot,
          adapter_rank, q_weight, v_weight, q_down, v_down, q_up, v_up)
    )


def solution(mesh):
    dims = factors(mesh.shape["wide"]) + (mesh.shape["tp"],)
    return jax.shard_map(
        functools.partial(local, dims),
        mesh=mesh,
        in_specs=(
            P("wide", None, None),
            P("wide", None, "tp"),
            P("wide", "tp", None, None),
            P("wide", "tp", None, None),
            P("wide"),
            P("wide"),
            P(),
            P(),
            P(None, "tp"),
            P(None, "tp"),
            P("wide", "tp", None),
            P("wide", "tp", None),
            P("wide", None, "tp"),
            P("wide", None, "tp"),
        ),
        out_specs=(P("wide", None, "tp"), P("wide", None, "tp")),
        check_vma=False,
    )
```

```python
import functools
import math

import jax
import jax.numpy as jnp
from jax import lax
from jax.experimental import pallas as pl
from jax.experimental.pallas import tpu as pltpu
from jax.sharding import PartitionSpec as P

MESH = pl.DeviceIdType.MESH
LANES = 128


def factors(wide):
    return (4, 4, wide // 16) if wide >= 32 else (1, 4, wide // 4)


def kernel(
    dims,
    hidden,
    new_keys,
    key_cache,
    value_cache,
    cache_len,
    adapter_id,
    adapter_slot,
    adapter_rank,
    q_weight,
    v_weight,
    q_down,
    v_down,
    q_up,
    v_up,
    attended,
    new_values,
    hid,
    hid_part,
    h32,
    h16,
    kv,
    vv,
    nk,
    len_s,
    id_s,
    slot_s,
    rank_s,
    wq,
    wv,
    down,
    upq,
    upv,
    own,
    feats,
    mixed,
    arrive_p,
    red,
    delta,
    back,
    far_out,
    far_in,
    base,
    cos_t,
    sin_t,
    kn,
    vn,
    local_sem,
    f_send,
    f_recv,
    n_send,
    n_recv,
    rs_send,
    rs_recv,
    ag_send,
    ag_recv,
    b_send,
    b_recv,
    r_send,
    r_recv,
):
    ny, nn, nf, nt = dims
    near = ny * nn
    rows, _, width = hidden.shape
    toks = rows * 2
    part = width // nt
    slots = q_up.shape[0]
    rank_w = q_up.shape[1]
    q_w = q_up.shape[2]
    v_w = v_up.shape[2]
    cache = key_cache.shape[2]
    adapters = adapter_slot.shape[0]
    chunk = near * toks
    piece = chunk // nt
    bf, f32 = jnp.bfloat16, jnp.float32

    wide = lax.axis_index("wide")
    tp = lax.axis_index("tp")
    nz = nf * nn
    y = lax.div(wide, nz)
    z = lax.rem(wide, nz)

    def turn(i, d, n):
        return lax.rem(i + d, n)

    def f_peer(d):
        return (y * nz + turn(z, d * nn + 2, nz), tp)

    even = lax.rem(z, 2) == 0
    steps = (0, 1, jnp.where(even, 2, nz - 2), nz - 1) if nn == 4 else (0, jnp.where(even, 1, nz - 1))
    homes = tuple(nz - s if i == 2 else s for i, s in enumerate(steps))

    def n_peer(e):
        return (turn(y, e // nn, ny) * nz + turn(z, steps[e % nn], nz), tp)

    def h_peer(e):
        return (turn(y, e // nn, ny) * nz + turn(z, homes[e % nn], nz), tp)

    def t_peer(e):
        return (wide, turn(tp, e, nt))

    def n_back(e):
        return (-(e // nn) % ny) * nn + (-(e % nn)) % nn

    order = sorted(range(nf), key=lambda d: min(d * nn + 2, nz - d * nn - 2))
    near_order = sorted(
        range(1, near), key=lambda e: -min(e // nn, ny - e // nn) - min(e % nn, nn - e % nn)
    )
    tp_order = sorted(range(1, nt), key=lambda e: -min(e, nt - e))

    loads = {}

    def load(name, src, dst, i):
        c = pltpu.make_async_copy(src, dst, local_sem.at[i])
        c.start()
        loads[name] = c

    def loaded(name):
        loads.pop(name).wait()

    col = pl.multiple_of(tp * part, part)
    load("hp", hidden.at[:, :, pl.ds(col, part)], hid_part, 0)
    load("id", adapter_id, id_s, 1)
    load("slot", adapter_slot, slot_s, 2)
    load("rank", adapter_rank, rank_s, 3)

    barrier = pltpu.get_barrier_semaphore()
    peers = (
        [f_peer(d) for d in order[::-1]]
        + [n_peer(e) for e in near_order]
        + [h_peer(e) for e in near_order if e % nn == 2]
        + [t_peer(e) for e in tp_order]
    )
    for p in peers:
        pl.semaphore_signal(barrier, inc=1, device_id=p, device_id_type=MESH)

    for name in ("id", "slot", "rank"):
        loaded(name)
    tok = lax.broadcasted_iota(jnp.int32, (toks, LANES), 0)
    lane = lax.broadcasted_iota(jnp.int32, (toks, LANES), 1)
    code = jnp.zeros((toks, LANES), jnp.int32)
    for r in range(rows):
        ident = id_s[r]
        mine = jnp.where(lax.rem(lane, rank_w) < rank_s[ident], slot_s[ident], adapters)
        code = jnp.where(lax.div(tok, 2) == r, mine, code)
    own[:, part:] = code.astype(f32).astype(bf)
    loaded("hp")
    for r in range(rows):
        h32[2 * r : 2 * r + 2, :part] = hid_part[r].astype(f32)
    own[:, :part] = h32[:, :part].astype(bf)

    def send(src, dst, ssem, rsem, peer):
        pltpu.make_async_remote_copy(
            src_ref=src,
            dst_ref=dst,
            send_sem=ssem,
            recv_sem=rsem,
            device_id=peer,
            device_id_type=MESH,
        ).start()

    def passed(ref, sem):
        pltpu.make_async_copy(ref, ref, sem).wait()

    pl.semaphore_wait(barrier, len(peers))

    for d in order[::-1]:
        there = nf - 1 - d
        send(own, feats.at[there, 0], f_send.at[d], f_recv.at[there], f_peer(d))

    def spread_near(d):
        passed(feats.at[d, 0], f_recv.at[d])
        for e in near_order:
            send(feats.at[d, 0], feats.at[d, n_back(e)], n_send.at[d], n_recv.at[d], n_peer(e))

    def products(d):
        passed(feats.at[d, pl.ds(1, near - 1)], n_recv.at[d])
        x = feats[d, :, :, :part].reshape(chunk, part)
        place = feats[d, :, :, part:].reshape(chunk, LANES).astype(f32)
        place = place - (wide * slots).astype(f32)
        prod = lax.dot_general(x, down[...], (((1,), (1,)), ((), ())), preferred_element_type=f32)
        total = jnp.zeros((chunk, LANES), f32)
        for k in range(slots):
            total = jnp.where(place == float(k), prod[:, k * LANES : (k + 1) * LANES], total)
        mixed[d] = total.reshape(nt, piece, LANES)
        for e in tp_order:
            send(
                mixed.at[d, turn(tp, e, nt)],
                arrive_p.at[d, nt - e],
                rs_send.at[d],
                rs_recv.at[d],
                t_peer(e),
            )

    def reduce(d):
        passed(arrive_p.at[d, pl.ds(1, nt - 1)], rs_recv.at[d])
        total = mixed[d, tp]
        for e in range(1, nt):
            total = total + arrive_p[d, e]
        red[d, 0] = total.astype(bf)
        for e in tp_order:
            send(red.at[d, 0], red.at[d, nt - e], ag_send.at[d], ag_recv.at[d], t_peer(e))

    def expand(d):
        passed(red.at[d, pl.ds(1, nt - 1)], ag_recv.at[d])
        shrunk = jnp.concatenate(
            [red[d, turn(nt - tp, p, nt)].astype(f32) for p in range(nt)], 0
        )
        place = feats[d, :, :, part:].reshape(chunk, LANES).astype(f32)
        place = place - (wide * slots).astype(f32)
        spread = jnp.concatenate(
            [jnp.where(place == float(k), shrunk, 0.0).astype(bf) for k in range(slots)], 1
        )
        dq = jnp.dot(spread, upq[...], preferred_element_type=f32).astype(bf)
        dv = jnp.dot(spread, upv[...], preferred_element_type=f32).astype(bf)
        delta[d, :, :, :q_w] = dq.reshape(near, toks, q_w)
        delta[d, :, :, q_w:] = dv.reshape(near, toks, v_w)
        for e in near_order:
            send(delta.at[d, e], back.at[d, n_back(e)], b_send.at[d], b_recv.at[d], h_peer(e))

    def gather_back(d):
        passed(back.at[d, pl.ds(1, near - 1)], b_recv.at[d])
        total = delta[d, 0].astype(f32) + jnp.sum(back[d, 1:].astype(f32), 0)
        far_out[d] = total.astype(bf)
        there = nf - 1 - d
        send(far_out.at[d], far_in.at[there], r_send.at[d], r_recv.at[there], f_peer(d))

    load("hid", hidden, hid, 0)
    load("len", cache_len, len_s, 4)
    load("nk", new_keys, nk, 5)
    for k in range(slots):
        row = k * 2 * rank_w
        load(f"qd{k}", q_down.at[k], down.at[pl.ds(row, rank_w)], 8 + 4 * k)
        load(f"vd{k}", v_down.at[k], down.at[pl.ds(row + rank_w, rank_w)], 9 + 4 * k)
    load("wq", q_weight, wq, 6)
    load("wv", v_weight, wv, 7)
    upq[...] = jnp.zeros_like(upq)
    upv[...] = jnp.zeros_like(upv)
    for k in range(slots):
        row = k * 2 * rank_w
        load(f"qu{k}", q_up.at[k], upq.at[pl.ds(row, rank_w)], 10 + 4 * k)
        load(f"vu{k}", v_up.at[k], upv.at[pl.ds(row + rank_w, rank_w)], 11 + 4 * k)
    n0 = 8 + 4 * slots
    load("kc", key_cache, kv, n0)
    load("vc", value_cache, vv, n0 + 1)
    loaded("hid")
    for r in range(rows):
        h32[2 * r : 2 * r + 2, :] = hid[r].astype(f32)
    h16[...] = h32[...].astype(bf)
    loaded("len")
    position = lax.rem(tok, 2)
    for r in range(rows):
        position = position + jnp.where(lax.div(tok, 2) == r, len_s[r], 0)
    half = lax.rem(lane, 64)
    frequency = jnp.exp(-math.log(500000.0) * (2.0 * half.astype(f32) / 128))
    angle = position.astype(f32) * frequency
    cos_t[...] = jnp.cos(angle)
    sine = jnp.sin(angle)
    sin_t[...] = jnp.where(lane < 64, -sine, sine)
    kn[...] = jnp.zeros_like(kn)
    vn[...] = jnp.zeros_like(vn)
    loaded("nk")
    for r in range(rows):
        kn[2 * r : 2 * r + 2, :] = nk[r].astype(f32)

    for d in order:
        spread_near(d)
    for name in ("wq", "wv"):
        loaded(name)
    base[:, :q_w] = jnp.dot(h16[...], wq[...], preferred_element_type=f32)
    for k in range(slots):
        loaded(f"qd{k}")
        loaded(f"vd{k}")
    for d in order:
        products(d)
    base[:, q_w:] = jnp.dot(h16[...], wv[...], preferred_element_type=f32)
    for k in range(slots):
        loaded(f"qu{k}")
        loaded(f"vu{k}")
    for d in order:
        reduce(d)
    for d in order:
        expand(d)
    loaded("kc")
    loaded("vc")
    for d in order:
        gather_back(d)
    for d in range(nf):
        passed(own, f_send.at[d])
        passed(feats.at[d, pl.ds(1, near - 1)], n_send.at[d])
        passed(arrive_p.at[d, pl.ds(1, nt - 1)], rs_send.at[d])
        passed(red.at[d, pl.ds(1, nt - 1)], ag_send.at[d])
        passed(back.at[d, pl.ds(1, near - 1)], b_send.at[d])
    total = jnp.zeros((toks, q_w + v_w), f32)
    for d in order:
        passed(far_in.at[d], r_recv.at[d])
        total = total + far_in[d].astype(f32)

    full = base[...] + total
    fresh = full[:, q_w:].astype(bf).astype(f32)
    vn[:toks, :] = fresh
    for r in range(rows):
        new_values[r] = fresh[2 * r : 2 * r + 2].astype(bf)
    heads = q_w // LANES
    turned = []
    for h in range(heads):
        x = full[:, h * LANES : (h + 1) * LANES]
        turned.append(x * cos_t[...] + pltpu.roll(x, 64, 1) * sin_t[...])
    queries = jnp.concatenate(turned, 0).astype(bf)
    many = heads * toks
    inv_root = 1.0 / math.sqrt(LANES)
    row_id = lax.broadcasted_iota(jnp.int32, (many, cache), 0)
    row_of = lax.div(lax.rem(row_id, toks), 2)
    spot = lax.broadcasted_iota(jnp.int32, (many, cache), 1)
    contract = (((1,), (1,)), ((), ()))
    scores = jnp.zeros((many, cache), f32)
    length = jnp.zeros((many, cache), jnp.int32)
    for r in range(rows):
        one = lax.dot_general(queries, kv[r, 0], contract, preferred_element_type=f32)
        scores = jnp.where(row_of == r, one, scores)
        length = jnp.where(row_of == r, len_s[r], length)
    scores = jnp.where(spot < length, scores * inv_root, -jnp.inf)
    fresh_scores = (
        lax.dot_general(queries, kn[...].astype(bf), contract, preferred_element_type=f32)
        * inv_root
    )
    row_n = lax.rem(lax.broadcasted_iota(jnp.int32, fresh_scores.shape, 0), toks)
    col_n = lax.broadcasted_iota(jnp.int32, fresh_scores.shape, 1)
    seen = (lax.div(row_n, 2) == lax.div(col_n, 2)) & (lax.rem(col_n, 2) <= lax.rem(row_n, 2))
    fresh_scores = jnp.where(seen, fresh_scores, -jnp.inf)
    largest = jnp.maximum(
        jnp.max(scores, -1, keepdims=True), jnp.max(fresh_scores, -1, keepdims=True)
    )
    old_weight = jnp.exp(scores - largest)
    new_weight = jnp.exp(fresh_scores - largest)
    denominator = jnp.sum(old_weight, -1, keepdims=True) + jnp.sum(new_weight, -1, keepdims=True)
    old_prob = old_weight / denominator
    new_prob = (new_weight / denominator).astype(bf)
    result = jnp.dot(new_prob, vn[...].astype(bf), preferred_element_type=f32)
    for r in range(rows):
        weights = jnp.where(row_of == r, old_prob, 0.0).astype(bf)
        result = result + jnp.dot(weights, vv[r, 0], preferred_element_type=f32)
    for r in range(rows):
        for h in range(heads):
            at = h * toks + 2 * r
            attended[r, :, h * LANES : (h + 1) * LANES] = result[at : at + 2].astype(bf)
    for d in order:
        passed(far_out.at[d], r_send.at[d])


def local(dims, *args):
    (hidden, new_keys, key_cache, value_cache, cache_len, adapter_id, adapter_slot, adapter_rank,
     q_weight, v_weight, q_down, v_down, q_up, v_up) = args
    ny, nn, nf, nt = dims
    near = ny * nn
    rows, _, width = hidden.shape
    toks = rows * 2
    part = width // nt
    slots, rank_w, q_w = q_up.shape
    v_w = v_up.shape[2]
    all_w = q_w + v_w
    piece = near * toks // nt
    bf, f32, i32 = jnp.bfloat16, jnp.float32, jnp.int32
    V = pltpu.VMEM
    dma = pltpu.SemaphoreType.DMA
    q_down = jnp.swapaxes(q_down, 1, 2)
    v_down = jnp.swapaxes(v_down, 1, 2)
    scratch = [
        V((rows, 2, width), bf),
        V((rows, 2, part), bf),
        V((toks, width), f32),
        V((toks, width), bf),
        V(key_cache.shape, bf),
        V(value_cache.shape, bf),
        V(new_keys.shape, bf),
        pltpu.SMEM(cache_len.shape, i32),
        pltpu.SMEM(adapter_id.shape, i32),
        pltpu.SMEM(adapter_slot.shape, i32),
        pltpu.SMEM(adapter_rank.shape, i32),
        V(q_weight.shape, bf),
        V(v_weight.shape, bf),
        V((slots * 2 * rank_w, part), bf),
        V((slots * 2 * rank_w, q_w), bf),
        V((slots * 2 * rank_w, v_w), bf),
        V((toks, part + LANES), bf),
        V((nf, near, toks, part + LANES), bf),
        V((nf, nt, piece, LANES), f32),
        V((nf, nt, piece, LANES), f32),
        V((nf, nt, piece, LANES), bf),
        V((nf, near, toks, all_w), bf),
        V((nf, near, toks, all_w), bf),
        V((nf, toks, all_w), bf),
        V((nf, toks, all_w), bf),
        V((toks, all_w), f32),
        V((toks, LANES), f32),
        V((toks, LANES), f32),
        V((LANES, LANES), f32),
        V((LANES, LANES), f32),
        dma((8 + 4 * slots + 2,)),
    ]
    scratch += [dma((nf,)) for _ in range(12)]
    any_space = pl.BlockSpec(memory_space=pl.ANY)
    vmem = pl.BlockSpec(memory_space=pltpu.VMEM)
    return tuple(
        pl.pallas_call(
            functools.partial(kernel, dims),
            out_shape=(
                jax.ShapeDtypeStruct((rows, 2, q_w), bf),
                jax.ShapeDtypeStruct((rows, 2, v_w), bf),
            ),
            in_specs=[any_space] * 14,
            out_specs=(vmem, vmem),
            scratch_shapes=scratch,
            compiler_params=pltpu.CompilerParams(
                collective_id=0, has_side_effects=True, vmem_limit_bytes=56 * 1024 * 1024
            ),
        )(hidden, new_keys, key_cache, value_cache, cache_len, adapter_id, adapter_slot,
          adapter_rank, q_weight, v_weight, q_down, v_down, q_up, v_up)
    )


def solution(mesh):
    dims = factors(mesh.shape["wide"]) + (mesh.shape["tp"],)
    return jax.shard_map(
        functools.partial(local, dims),
        mesh=mesh,
        in_specs=(
            P("wide", None, None),
            P("wide", None, "tp"),
            P("wide", "tp", None, None),
            P("wide", "tp", None, None),
            P("wide"),
            P("wide"),
            P(),
            P(),
            P(None, "tp"),
            P(None, "tp"),
            P("wide", "tp", None),
            P("wide", "tp", None),
            P("wide", None, "tp"),
            P("wide", None, "tp"),
        ),
        out_specs=(P("wide", None, "tp"), P("wide", None, "tp")),
        check_vma=False,
    )
```

```python
import functools
import math

import jax
import jax.numpy as jnp
from jax import lax
from jax.experimental import pallas as pl
from jax.experimental.pallas import tpu as pltpu
from jax.sharding import PartitionSpec as P

MESH = pl.DeviceIdType.MESH
LANES = 128


def factors(wide):
    return (4, 4, wide // 16) if wide >= 32 else (1, 4, wide // 4)


def kernel(
    dims,
    hidden,
    new_keys,
    key_cache,
    value_cache,
    cache_len,
    adapter_id,
    adapter_slot,
    adapter_rank,
    q_weight,
    v_weight,
    q_down,
    v_down,
    q_up,
    v_up,
    attended_out,
    new_values_out,
    attended,
    new_values,
    hid,
    hid_part,
    h32,
    h16,
    kv,
    vv,
    nk,
    len_s,
    id_s,
    slot_s,
    rank_s,
    wq,
    wv,
    down,
    upq,
    upv,
    own,
    feats,
    mixed,
    arrive_p,
    red,
    delta,
    back,
    far_out,
    far_in,
    base,
    cos_t,
    sin_t,
    kn,
    vn,
    local_sem,
    f_send,
    f_recv,
    n_send,
    n_recv,
    rs_send,
    rs_recv,
    ag_send,
    ag_recv,
    b_send,
    b_recv,
    r_send,
    r_recv,
):
    ny, nn, nf, nt = dims
    near = ny * nn
    rows, _, width = hidden.shape
    toks = rows * 2
    part = width // nt
    slots = q_up.shape[0]
    rank_w = q_up.shape[1]
    q_w = q_up.shape[2]
    v_w = v_up.shape[2]
    cache = key_cache.shape[2]
    adapters = adapter_slot.shape[0]
    chunk = near * toks
    piece = chunk // nt
    bf, f32 = jnp.bfloat16, jnp.float32

    wide = lax.axis_index("wide")
    tp = lax.axis_index("tp")
    nz = nf * nn
    y = lax.div(wide, nz)
    z = lax.rem(wide, nz)

    def turn(i, d, n):
        return lax.rem(i + d, n)

    def f_peer(d):
        return (y * nz + turn(z, d * nn + 2, nz), tp)

    even = lax.rem(z, 2) == 0
    steps = (0, 1, jnp.where(even, 2, nz - 2), nz - 1) if nn == 4 else (0, jnp.where(even, 1, nz - 1))
    homes = tuple(nz - s if i == 2 else s for i, s in enumerate(steps))

    def n_peer(e):
        return (turn(y, e // nn, ny) * nz + turn(z, steps[e % nn], nz), tp)

    def h_peer(e):
        return (turn(y, e // nn, ny) * nz + turn(z, homes[e % nn], nz), tp)

    def t_peer(e):
        return (wide, turn(tp, e, nt))

    def n_back(e):
        return (-(e // nn) % ny) * nn + (-(e % nn)) % nn

    order = sorted(range(nf), key=lambda d: min(d * nn + 2, nz - d * nn - 2))
    near_order = sorted(
        range(1, near), key=lambda e: -min(e // nn, ny - e // nn) - min(e % nn, nn - e % nn)
    )
    tp_order = sorted(range(1, nt), key=lambda e: -min(e, nt - e))

    loads = {}

    def load(name, src, dst, i):
        c = pltpu.make_async_copy(src, dst, local_sem.at[i])
        c.start()
        loads[name] = c

    def loaded(name):
        loads.pop(name).wait()

    col = pl.multiple_of(tp * part, part)
    load("hp", hidden.at[:, :, pl.ds(col, part)], hid_part, 0)
    load("id", adapter_id, id_s, 1)
    load("slot", adapter_slot, slot_s, 2)
    load("rank", adapter_rank, rank_s, 3)

    barrier = pltpu.get_barrier_semaphore()
    peers = (
        [f_peer(d) for d in order[::-1]]
        + [n_peer(e) for e in near_order]
        + [h_peer(e) for e in near_order if e % nn == 2]
        + [t_peer(e) for e in tp_order]
    )
    for p in peers:
        pl.semaphore_signal(barrier, inc=1, device_id=p, device_id_type=MESH)

    for name in ("id", "slot", "rank"):
        loaded(name)
    tok = lax.broadcasted_iota(jnp.int32, (toks, LANES), 0)
    lane = lax.broadcasted_iota(jnp.int32, (toks, LANES), 1)
    code = jnp.zeros((toks, LANES), jnp.int32)
    for r in range(rows):
        ident = id_s[r]
        mine = jnp.where(lax.rem(lane, rank_w) < rank_s[ident], slot_s[ident], adapters)
        code = jnp.where(lax.div(tok, 2) == r, mine, code)
    own[:, part:] = code.astype(f32).astype(bf)
    loaded("hp")
    for r in range(rows):
        h32[2 * r : 2 * r + 2, :part] = hid_part[r].astype(f32)
    own[:, :part] = h32[:, :part].astype(bf)

    def send(src, dst, ssem, rsem, peer):
        pltpu.make_async_remote_copy(
            src_ref=src,
            dst_ref=dst,
            send_sem=ssem,
            recv_sem=rsem,
            device_id=peer,
            device_id_type=MESH,
        ).start()

    def passed(ref, sem):
        pltpu.make_async_copy(ref, ref, sem).wait()

    pl.semaphore_wait(barrier, len(peers))

    for d in order[::-1]:
        there = nf - 1 - d
        send(own, feats.at[there, 0], f_send.at[d], f_recv.at[there], f_peer(d))

    def spread_near(d):
        passed(feats.at[d, 0], f_recv.at[d])
        for e in near_order:
            send(feats.at[d, 0], feats.at[d, n_back(e)], n_send.at[d], n_recv.at[d], n_peer(e))

    def products(d):
        passed(feats.at[d, pl.ds(1, near - 1)], n_recv.at[d])
        x = feats[d, :, :, :part].reshape(chunk, part)
        place = feats[d, :, :, part:].reshape(chunk, LANES).astype(f32)
        place = place - (wide * slots).astype(f32)
        prod = lax.dot_general(x, down[...], (((1,), (1,)), ((), ())), preferred_element_type=f32)
        total = jnp.zeros((chunk, LANES), f32)
        for k in range(slots):
            total = jnp.where(place == float(k), prod[:, k * LANES : (k + 1) * LANES], total)
        mixed[d] = total.reshape(nt, piece, LANES)
        for e in tp_order:
            send(
                mixed.at[d, turn(tp, e, nt)],
                arrive_p.at[d, nt - e],
                rs_send.at[d],
                rs_recv.at[d],
                t_peer(e),
            )

    def reduce(d):
        passed(arrive_p.at[d, pl.ds(1, nt - 1)], rs_recv.at[d])
        total = mixed[d, tp]
        for e in range(1, nt):
            total = total + arrive_p[d, e]
        red[d, 0] = total.astype(bf)
        for e in tp_order:
            send(red.at[d, 0], red.at[d, nt - e], ag_send.at[d], ag_recv.at[d], t_peer(e))

    def expand(d):
        passed(red.at[d, pl.ds(1, nt - 1)], ag_recv.at[d])
        shrunk = jnp.concatenate(
            [red[d, turn(nt - tp, p, nt)].astype(f32) for p in range(nt)], 0
        )
        place = feats[d, :, :, part:].reshape(chunk, LANES).astype(f32)
        place = place - (wide * slots).astype(f32)
        spread = jnp.concatenate(
            [jnp.where(place == float(k), shrunk, 0.0).astype(bf) for k in range(slots)], 1
        )
        dq = jnp.dot(spread, upq[...], preferred_element_type=f32).astype(bf)
        dv = jnp.dot(spread, upv[...], preferred_element_type=f32).astype(bf)
        delta[d, :, :, :q_w] = dq.reshape(near, toks, q_w)
        delta[d, :, :, q_w:] = dv.reshape(near, toks, v_w)
        for e in near_order:
            send(delta.at[d, e], back.at[d, n_back(e)], b_send.at[d], b_recv.at[d], h_peer(e))

    def gather_back(d):
        passed(back.at[d, pl.ds(1, near - 1)], b_recv.at[d])
        total = delta[d, 0].astype(f32) + jnp.sum(back[d, 1:].astype(f32), 0)
        far_out[d] = total.astype(bf)
        there = nf - 1 - d
        send(far_out.at[d], far_in.at[there], r_send.at[d], r_recv.at[there], f_peer(d))

    load("hid", hidden, hid, 0)
    load("len", cache_len, len_s, 4)
    load("nk", new_keys, nk, 5)
    for k in range(slots):
        row = k * 2 * rank_w
        load(f"qd{k}", q_down.at[k], down.at[pl.ds(row, rank_w)], 8 + 4 * k)
        load(f"vd{k}", v_down.at[k], down.at[pl.ds(row + rank_w, rank_w)], 9 + 4 * k)
    load("wq", q_weight, wq, 6)
    load("wv", v_weight, wv, 7)
    upq[...] = jnp.zeros_like(upq)
    upv[...] = jnp.zeros_like(upv)
    for k in range(slots):
        row = k * 2 * rank_w
        load(f"qu{k}", q_up.at[k], upq.at[pl.ds(row, rank_w)], 10 + 4 * k)
        load(f"vu{k}", v_up.at[k], upv.at[pl.ds(row + rank_w, rank_w)], 11 + 4 * k)
    n0 = 8 + 4 * slots
    load("kc", key_cache, kv, n0)
    load("vc", value_cache, vv, n0 + 1)
    loaded("hid")
    for r in range(rows):
        h32[2 * r : 2 * r + 2, :] = hid[r].astype(f32)
    h16[...] = h32[...].astype(bf)
    loaded("len")
    position = lax.rem(tok, 2)
    for r in range(rows):
        position = position + jnp.where(lax.div(tok, 2) == r, len_s[r], 0)
    half = lax.rem(lane, 64)
    frequency = jnp.exp(-math.log(500000.0) * (2.0 * half.astype(f32) / 128))
    angle = position.astype(f32) * frequency
    cos_t[...] = jnp.cos(angle)
    sine = jnp.sin(angle)
    sin_t[...] = jnp.where(lane < 64, -sine, sine)
    kn[...] = jnp.zeros_like(kn)
    vn[...] = jnp.zeros_like(vn)
    loaded("nk")
    for r in range(rows):
        kn[2 * r : 2 * r + 2, :] = nk[r].astype(f32)

    for d in order:
        spread_near(d)
    for name in ("wq", "wv"):
        loaded(name)
    base[:, :q_w] = jnp.dot(h16[...], wq[...], preferred_element_type=f32)
    for k in range(slots):
        loaded(f"qd{k}")
        loaded(f"vd{k}")
    for d in order:
        products(d)
    base[:, q_w:] = jnp.dot(h16[...], wv[...], preferred_element_type=f32)
    for k in range(slots):
        loaded(f"qu{k}")
        loaded(f"vu{k}")
    for d in order:
        reduce(d)
    for d in order:
        expand(d)
    loaded("kc")
    loaded("vc")
    for d in order:
        gather_back(d)
    for d in range(nf):
        passed(own, f_send.at[d])
        passed(feats.at[d, pl.ds(1, near - 1)], n_send.at[d])
        passed(arrive_p.at[d, pl.ds(1, nt - 1)], rs_send.at[d])
        passed(red.at[d, pl.ds(1, nt - 1)], ag_send.at[d])
        passed(back.at[d, pl.ds(1, near - 1)], b_send.at[d])
    total = jnp.zeros((toks, q_w + v_w), f32)
    for d in order:
        passed(far_in.at[d], r_recv.at[d])
        total = total + far_in[d].astype(f32)

    full = base[...] + total
    fresh = full[:, q_w:].astype(bf).astype(f32)
    vn[:toks, :] = fresh
    for r in range(rows):
        new_values[r] = fresh[2 * r : 2 * r + 2].astype(bf)
    load("nv", new_values, new_values_out, 0)
    heads = q_w // LANES
    turned = []
    for h in range(heads):
        x = full[:, h * LANES : (h + 1) * LANES]
        turned.append(x * cos_t[...] + pltpu.roll(x, 64, 1) * sin_t[...])
    queries = jnp.concatenate(turned, 0).astype(bf)
    many = heads * toks
    inv_root = 1.0 / math.sqrt(LANES)
    row_id = lax.broadcasted_iota(jnp.int32, (many, cache), 0)
    row_of = lax.div(lax.rem(row_id, toks), 2)
    spot = lax.broadcasted_iota(jnp.int32, (many, cache), 1)
    contract = (((1,), (1,)), ((), ()))
    scores = jnp.zeros((many, cache), f32)
    length = jnp.zeros((many, cache), jnp.int32)
    for r in range(rows):
        one = lax.dot_general(queries, kv[r, 0], contract, preferred_element_type=f32)
        scores = jnp.where(row_of == r, one, scores)
        length = jnp.where(row_of == r, len_s[r], length)
    scores = jnp.where(spot < length, scores * inv_root, -jnp.inf)
    fresh_scores = (
        lax.dot_general(queries, kn[...].astype(bf), contract, preferred_element_type=f32)
        * inv_root
    )
    row_n = lax.rem(lax.broadcasted_iota(jnp.int32, fresh_scores.shape, 0), toks)
    col_n = lax.broadcasted_iota(jnp.int32, fresh_scores.shape, 1)
    seen = (lax.div(row_n, 2) == lax.div(col_n, 2)) & (lax.rem(col_n, 2) <= lax.rem(row_n, 2))
    fresh_scores = jnp.where(seen, fresh_scores, -jnp.inf)
    largest = jnp.maximum(
        jnp.max(scores, -1, keepdims=True), jnp.max(fresh_scores, -1, keepdims=True)
    )
    old_weight = jnp.exp(scores - largest)
    new_weight = jnp.exp(fresh_scores - largest)
    denominator = jnp.sum(old_weight, -1, keepdims=True) + jnp.sum(new_weight, -1, keepdims=True)
    old_prob = old_weight / denominator
    new_prob = (new_weight / denominator).astype(bf)
    result = jnp.dot(new_prob, vn[...].astype(bf), preferred_element_type=f32)
    for r in range(rows):
        weights = jnp.where(row_of == r, old_prob, 0.0).astype(bf)
        result = result + jnp.dot(weights, vv[r, 0], preferred_element_type=f32)
    for r in range(rows):
        for h in range(heads):
            at = h * toks + 2 * r
            attended[r, :, h * LANES : (h + 1) * LANES] = result[at : at + 2].astype(bf)
    load("at", attended, attended_out, 1)
    for d in order:
        passed(far_out.at[d], r_send.at[d])
    loaded("nv")
    loaded("at")


def write_out(a, b, out_a, out_b, sems):
    copies = [
        pltpu.make_async_copy(a, out_a, sems.at[0]),
        pltpu.make_async_copy(b, out_b, sems.at[1]),
    ]
    for c in copies:
        c.start()
    for c in copies:
        c.wait()


def local(dims, *args):
    (hidden, new_keys, key_cache, value_cache, cache_len, adapter_id, adapter_slot, adapter_rank,
     q_weight, v_weight, q_down, v_down, q_up, v_up) = args
    ny, nn, nf, nt = dims
    near = ny * nn
    rows, _, width = hidden.shape
    toks = rows * 2
    part = width // nt
    slots, rank_w, q_w = q_up.shape
    v_w = v_up.shape[2]
    all_w = q_w + v_w
    piece = near * toks // nt
    bf, f32, i32 = jnp.bfloat16, jnp.float32, jnp.int32
    V = pltpu.VMEM
    dma = pltpu.SemaphoreType.DMA
    q_down = jnp.swapaxes(q_down, 1, 2)
    v_down = jnp.swapaxes(v_down, 1, 2)
    scratch = [
        V((rows, 2, q_w), bf),
        V((rows, 2, v_w), bf),
        V((rows, 2, width), bf),
        V((rows, 2, part), bf),
        V((toks, width), f32),
        V((toks, width), bf),
        V(key_cache.shape, bf),
        V(value_cache.shape, bf),
        V(new_keys.shape, bf),
        pltpu.SMEM(cache_len.shape, i32),
        pltpu.SMEM(adapter_id.shape, i32),
        pltpu.SMEM(adapter_slot.shape, i32),
        pltpu.SMEM(adapter_rank.shape, i32),
        V(q_weight.shape, bf),
        V(v_weight.shape, bf),
        V((slots * 2 * rank_w, part), bf),
        V((slots * 2 * rank_w, q_w), bf),
        V((slots * 2 * rank_w, v_w), bf),
        V((toks, part + LANES), bf),
        V((nf, near, toks, part + LANES), bf),
        V((nf, nt, piece, LANES), f32),
        V((nf, nt, piece, LANES), f32),
        V((nf, nt, piece, LANES), bf),
        V((nf, near, toks, all_w), bf),
        V((nf, near, toks, all_w), bf),
        V((nf, toks, all_w), bf),
        V((nf, toks, all_w), bf),
        V((toks, all_w), f32),
        V((toks, LANES), f32),
        V((toks, LANES), f32),
        V((LANES, LANES), f32),
        V((LANES, LANES), f32),
        dma((8 + 4 * slots + 2,)),
    ]
    scratch += [dma((nf,)) for _ in range(12)]
    any_space = pl.BlockSpec(memory_space=pl.ANY)
    shapes = (
        jax.ShapeDtypeStruct((rows, 2, q_w), bf),
        jax.ShapeDtypeStruct((rows, 2, v_w), bf),
    )
    outs = (
        pl.pallas_call(
            functools.partial(kernel, dims),
            out_shape=shapes,
            in_specs=[any_space] * 14,
            out_specs=(any_space, any_space),
            scratch_shapes=scratch,
            compiler_params=pltpu.CompilerParams(
                collective_id=0, has_side_effects=True, vmem_limit_bytes=56 * 1024 * 1024
            ),
        )(hidden, new_keys, key_cache, value_cache, cache_len, adapter_id, adapter_slot,
          adapter_rank, q_weight, v_weight, q_down, v_down, q_up, v_up)
    )
    return pl.pallas_call(
        write_out,
        out_shape=shapes,
        in_specs=[any_space] * 2,
        out_specs=(any_space, any_space),
        scratch_shapes=[dma((2,))],
        compiler_params=pltpu.CompilerParams(vmem_limit_bytes=56 * 1024 * 1024),
    )(*outs)


def solution(mesh):
    dims = factors(mesh.shape["wide"]) + (mesh.shape["tp"],)
    return jax.shard_map(
        functools.partial(local, dims),
        mesh=mesh,
        in_specs=(
            P("wide", None, None),
            P("wide", None, "tp"),
            P("wide", "tp", None, None),
            P("wide", "tp", None, None),
            P("wide"),
            P("wide"),
            P(),
            P(),
            P(None, "tp"),
            P(None, "tp"),
            P("wide", "tp", None),
            P("wide", "tp", None),
            P("wide", None, "tp"),
            P("wide", None, "tp"),
        ),
        out_specs=(P("wide", None, "tp"), P("wide", None, "tp")),
        check_vma=False,
    )
```
